128 devices in a mesh: grp: 4 (over x), dev: 32 (over z, y, core).
Axes of the slice: x: 4, y: 4, z: 4, core: 2. Of those that a mesh axis runs over, the one named last changes fastest.
Arguments:
- tracers: float32 [72, 8, 32, 4096], P(None, None, 'grp', 'dev'), may hold values from -6 to 6
- wind_east: float32 [72, 32, 4096], P(None, 'grp', 'dev'), may hold values from -1 to 1
- wind_north: float32 [72, 32, 4096], P(None, 'grp', 'dev'), may hold values from -1 to 1
- point_mass: float32 [32, 4096], P('grp', 'dev'), may hold values from 0.5 to 2
- diffusivity: float32 [72, 128, 2048], P(None, ('grp', 'dev')), may hold values from 0.05 to 2000
- destination: int32 [128, 1024, 1], P(('grp', 'dev')), may hold values from 0 to 127; in each aligned block of 1024 rows (0 to 1023, 1024 to 2047, ..., all dimensions but the last counted through in order) at most 16 rows name the same one
- column_cost: int32 [128, 1024], P(('grp', 'dev')), may hold values from 1 to 3
Outputs:
- mixed_tracers: float32 [72, 8, 32, 4096], P(None, None, 'grp', 'dev')
- bottom_values: float32 [8, 128, 2048], P(None, ('grp', 'dev'))
The draws below stay inside these ranges and needn't reach their ends.
Inputs may be any that keep to these rules, and one draw needn't show every extreme that they name: `destination`: each owner sends at most 16 of its columns to one physics device, and in every draw some owner sends exactly 16 to one device.
All inputs are finite; a program needn't handle non-finite values.
Results may differ from the reference program's by a relative error of at most 0.0003.
Values sent between devices are 32-bit elements; how exact they have to be, the bound alone decides.
A program may use at most 128 MiB of HBM per device.

```python
import math
import jax
import jax.numpy as jnp
import numpy as np
from jax import lax

TRACERS = 8
LEV = 72
SUBSTEPS = 3
PXL = 8
PYL = 128
COLS_DEV = 1024
NX = 32
NY = 4096
CAP = 16
SLOTS = 2048
N_GRP = 4
N_DEV = 32
DEVICES = 128


def loguniform_field(key, shape, low_end, high_end):
    unit = jax.random.uniform(key, shape, jnp.float32)
    return jnp.exp(jnp.log(low_end) + unit * (jnp.log(high_end) - jnp.log(low_end)))


def draw_diffusivity(key, part):
    key = jax.random.fold_in(key, 11)
    key_column = jax.random.fold_in(key, 1)
    key_level = jax.random.fold_in(key, 2)
    column_scale = loguniform_field(key_column, (1, DEVICES, SLOTS), 0.1, 400.0)
    level_factor = loguniform_field(key_level, (LEV, DEVICES, SLOTS), 0.5, 2.0)
    return (column_scale * level_factor).astype(jnp.float32)


def set_ends(values, key, low, high):
    extent = values.shape
    index_at = [jax.random.randint(jax.random.fold_in(key, axis), (), 0, extent[axis]) for axis in range(len(extent))]
    values = values.at[tuple(index_at)].set(low)
    longest = extent.index(max(extent))
    index_at[longest] = (index_at[longest] + 1) % extent[longest]
    return values.at[tuple(index_at)].set(high)


def block_scale(stream_key, dims, shards, smallest, top_value):
    def one(dim, blocks):
        heights = jax.random.uniform(jax.random.fold_in(jax.random.fold_in(stream_key, 6), dim), (blocks,), jnp.float32, smallest / len(shards), top_value / len(shards))
        return jnp.repeat(jnp.exp(heights), dims[dim] // blocks).reshape((-1,) + (1,) * (len(dims) - dim - 1))

    factor_of = one(*shards[0])
    for cut in shards[1:]:
        factor_of = factor_of * one(*cut)
    return factor_of


def deal_out(key, own, number, rows, amount, top, bound, skew):
    sequence = jax.random.permutation(key, amount)
    heavy_load, ordinary = portions_of(amount, rows * top, bound, skew, True), portions_of(amount, rows * top, bound, skew, False)
    places = jnp.arange(amount)

    def named(sizes, turn):
        used = int((sizes > 0).sum())
        fixed = max(1, used // 4)
        shifted = fixed + (places - fixed + turn * (used - fixed)) % max(1, amount - fixed)
        return jnp.zeros((amount,), jnp.int32).at[sequence[jnp.where(places < fixed, places, shifted)]].set(jnp.asarray(sizes, jnp.int32))

    sizes = jnp.where(number % 4 == 0, named(heavy_load, number // 4), named(ordinary, number - number // 4 - 1))
    mixed = jax.random.permutation(jax.random.fold_in(own, 3), amount)
    source_of, receiver = mixed[0:amount // 2 * 2:2], mixed[1:amount // 2 * 2:2]
    room = jnp.minimum(sizes[source_of] - 1, bound - sizes[receiver]) // 2
    room = jnp.where((source_of == sequence[0]) | (receiver == sequence[0]) | (sizes[receiver] == 0), 0, jnp.maximum(room, 0))
    shifted = jax.random.randint(jax.random.fold_in(own, 4), (amount // 2,), 0, 1 << 20) % (room + 1)
    sizes = sizes.at[source_of].add(-shifted).at[receiver].add(shifted)
    items = jnp.searchsorted(jnp.cumsum(sizes), jnp.arange(rows * top), side="right").astype(jnp.int32)
    grid = items.reshape(top, rows).T
    grid = grid[jax.random.permutation(jax.random.fold_in(own, 1), rows)]
    turn = jax.random.randint(jax.random.fold_in(own, 2), (rows, 1), 0, top)
    return jnp.take_along_axis(grid, (jnp.arange(top)[None, :] + turn) % top, axis=1)


def portions_of(number_of, total, bound, lean, full):
    weights = [(1 << 20) // math.isqrt(standing ** lean) + 1 for standing in range(1, number_of + 1)]
    largest = bound if full else min(bound, max(-(-total // number_of), total * weights[0] // sum(weights)))
    least = 1 if total - largest >= number_of - 1 else 0
    counts, spare = [largest] + [least] * (number_of - 1), total - largest - least * (number_of - 1)
    while spare > 0:
        movable = [i for i in range(1, number_of) if counts[i] < largest] or [i for i in range(1, number_of) if counts[i] < bound]
        mass, remaining = sum([weights[i] for i in movable]), spare
        for i in movable:
            more = min(bound - counts[i], max(1, remaining * weights[i] // mass), spare)
            counts[i] = counts[i] + more
            spare = spare - more
    return np.array(counts)


def gaussian(stream_key, extent, deviation, reach, pieces=(), kind=jnp.bfloat16):
    drawn = deviation * jax.random.normal(stream_key, extent, jnp.float32)
    if pieces:
        drawn = drawn * block_scale(stream_key, extent, pieces, -0.22, 0.18)
    return jnp.clip(drawn, -reach, reach).astype(kind)


def setup_inputs(seed: int = 0) -> dict:
    arg_keys = jax.random.split(jax.random.key(seed), 8)
    tracers = gaussian(arg_keys[0], (LEV, TRACERS, NX, NY), 1.0, 6.0, ((2, 4), (3, 32)), jnp.float32)
    wind_east = gaussian(arg_keys[1], (LEV, NX, NY), 0.15, 1.0, ((1, 4), (2, 32)), jnp.float32)
    wind_north = gaussian(arg_keys[2], (LEV, NX, NY), 0.15, 1.0, ((1, 4), (2, 32)), jnp.float32)
    point_mass = jnp.clip(jnp.exp(math.log(2.0) - 1.3862944 * jax.random.uniform(arg_keys[3], (NX, NY), jnp.float32) ** block_scale(arg_keys[3], (NX, NY), ((0, 4), (1, 32)), -0.2, 0.2)), 0.5, 2.0)
    diffusivity = draw_diffusivity(jax.random.fold_in(arg_keys[7], 71), 0)
    destination_keys = jax.random.split(jax.random.fold_in(arg_keys[5], 1), DEVICES * COLS_DEV // COLS_DEV)
    destination_turns = jax.random.permutation(jax.random.fold_in(arg_keys[5], 3), DEVICES * COLS_DEV // COLS_DEV)
    destination = jax.vmap(lambda own, number: deal_out(jax.random.fold_in(arg_keys[5], 2), own, number, COLS_DEV, DEVICES, 1, CAP, 2))(destination_keys, destination_turns).reshape((DEVICES, COLS_DEV, 1))
    column_cost = set_ends(jax.random.randint(arg_keys[6], (DEVICES, COLS_DEV), 1, 4), jax.random.fold_in(arg_keys[6], 1), 1, 3).astype(jnp.int32)
    return {"tracers": tracers, "wind_east": wind_east, "wind_north": wind_north, "point_mass": point_mass, "diffusivity": diffusivity, "destination": destination, "column_cost": column_cost}


def gll_derivative():
    points_gll = np.array([-1.0, -1.0 / np.sqrt(5.0), 1.0 / np.sqrt(5.0), 1.0])
    matrix_der = np.zeros((4, 4))
    for i in range(4):
        for k in range(4):
            if i == k:
                running = 0.0
                for m in range(4):
                    if m != k:
                        running += 1.0 / (points_gll[k] - points_gll[m])
                matrix_der[i, k] = running
            else:
                product_term = 1.0
                for m in range(4):
                    if m != k and m != i:
                        product_term *= (points_gll[i] - points_gll[m]) / (points_gll[k] - points_gll[m])
                matrix_der[i, k] = product_term / (points_gll[k] - points_gll[i])
    return matrix_der

def edge_sum(values, count_x, count_y):
    index_x = jnp.arange(count_x) % 4
    first_x = (index_x == 0).astype(jnp.float32)[:, None]
    last_x = (index_x == 3).astype(jnp.float32)[:, None]
    summed = values + first_x * jnp.roll(values, 1, axis=-2) + last_x * jnp.roll(values, -1, axis=-2)
    index_y = jnp.arange(count_y) % 4
    first_y = (index_y == 0).astype(jnp.float32)
    last_y = (index_y == 3).astype(jnp.float32)
    return summed + first_y * jnp.roll(summed, 1, axis=-1) + last_y * jnp.roll(summed, -1, axis=-1)

def factorize(kappa_cols):
    half_level = 0.5 * (kappa_cols[:-1] + kappa_cols[1:])
    zeros_row = jnp.zeros_like(kappa_cols[:1])
    below_coef = jnp.concatenate([zeros_row, half_level], axis=0)
    above_coef = jnp.concatenate([half_level, zeros_row], axis=0)

    def forward(previous, inputs):
        below_k, above_k = inputs
        inverse = 1.0 / (1.0 + below_k + above_k + below_k * previous)
        ratio_k = -above_k * inverse
        return (ratio_k, (ratio_k, inverse))
    _, (ratios, inverses) = lax.scan(forward, jnp.zeros_like(kappa_cols[0]), (below_coef, above_coef))
    return (below_coef, ratios, inverses)

def solve_column(profile, below_coef, ratios, inverses):

    def forward(previous, inputs):
        value_k, below_k, inverse = inputs
        current = (value_k + below_k * previous) * inverse
        return (current, current)
    _, reduced = lax.scan(forward, jnp.zeros_like(profile[0]), (profile, below_coef, inverses))

    def backward(following, inputs):
        value_k, ratio_k = inputs
        current = value_k - ratio_k * following
        return (current, current)
    _, result = lax.scan(backward, jnp.zeros_like(profile[0]), (reduced, ratios), reverse=True)
    return result

def mix_columns(profile, below_coef, ratios, inverses, solve_count):
    for substep in range(SUBSTEPS):
        updated = solve_column(profile, below_coef, ratios, inverses)
        profile = jnp.where(solve_count >= substep + 1, updated, profile)
    return profile

def owner_ranks(targets):
    matches = (targets[:, None] == jnp.arange(DEVICES, dtype=jnp.int32)[None, :]).astype(jnp.int32)
    before = jnp.cumsum(matches, axis=0) - matches
    return lax.optimization_barrier(jnp.sum(before * matches, axis=1)).astype(jnp.int32)

def reference(tracers, wind_east, wind_north, point_mass, diffusivity, destination, column_cost):
    matrix_der = jnp.asarray(gll_derivative(), dtype=jnp.float32)
    by_tracer = jnp.swapaxes(tracers, 0, 1)
    count_x = tracers.shape[2]
    count_y = tracers.shape[3]
    mass_sum = edge_sum(point_mass, count_x, count_y)
    owners = destination[:, :, 0].astype(jnp.int32)
    column_rank = lax.map(owner_ranks, owners)
    slot_index = (jnp.arange(DEVICES, dtype=jnp.int32)[:, None] * CAP + column_rank).astype(jnp.int32)
    kappa_cols = diffusivity[:, owners, slot_index]
    below_coef, ratios, inverses = factorize(kappa_cols)

    def one_tracer(values):
        blocks_x = values.reshape(LEV, count_x // 4, 4, count_y)
        deriv_east = jnp.einsum('ik,lakc->laic', matrix_der, blocks_x, precision=lax.Precision.HIGHEST).reshape(values.shape)
        blocks_y = values.reshape(LEV, count_x, count_y // 4, 4)
        deriv_north = jnp.einsum('ik,lxbk->lxbi', matrix_der, blocks_y, precision=lax.Precision.HIGHEST).reshape(values.shape)
        advected = values - (wind_east * deriv_east + wind_north * deriv_north)
        averaged = edge_sum(point_mass * advected, count_x, count_y) / mass_sum
        owned = averaged.reshape(LEV, N_GRP, PXL, N_DEV, PYL).transpose(0, 1, 3, 2, 4).reshape(LEV, DEVICES, COLS_DEV)
        mixed = mix_columns(owned, below_coef, ratios, inverses, column_cost)
        back_grid = mixed.reshape(LEV, N_GRP, N_DEV, PXL, PYL).transpose(0, 1, 3, 2, 4).reshape(LEV, count_x, count_y)
        return (back_grid, mixed[LEV - 1])
    mixed_tracers, bottoms = lax.map(one_tracer, by_tracer)
    bottom_values = jnp.zeros((tracers.shape[1], DEVICES, SLOTS), jnp.float32).at[:, owners, slot_index].set(bottoms)
    return (jnp.swapaxes(mixed_tracers, 0, 1), bottom_values)
```

```python
import jax
import jax.numpy as jnp
import numpy as np
from jax import lax
from jax.experimental import pallas as pl
from jax.experimental.pallas import tpu as pltpu
from jax.sharding import PartitionSpec as P

LEV = 72
TRC = 8
ROWS = LEV * TRC * 8
GRP = 4
DEV = 32
ALL = GRP * DEV
CUTS = ((0, 25), (25, 49), (49, 73))
MESH = pl.DeviceIdType.MESH
F32 = jnp.float32
BF16 = jnp.bfloat16


def gll_derivative():
    points = np.array([-1.0, -1.0 / np.sqrt(5.0), 1.0 / np.sqrt(5.0), 1.0])
    der = np.zeros((4, 4))
    for i in range(4):
        for k in range(4):
            others = [m for m in range(4) if m != k]
            if i == k:
                der[i, k] = sum(1.0 / (points[k] - points[m]) for m in others)
            else:
                term = 1.0
                for m in others:
                    if m != i:
                        term *= (points[i] - points[m]) / (points[k] - points[m])
                der[i, k] = term / (points[k] - points[i])
    return der


def north_weights():
    along = np.kron(np.eye(32), gll_derivative().T).astype(np.float32)
    high = along.astype(jnp.bfloat16)
    low = (along - high.astype(np.float32)).astype(jnp.bfloat16)
    return np.block([[high, low], [high, np.zeros_like(low)]])


def iota(shape, dim):
    return lax.broadcasted_iota(jnp.int32, shape, dim)


def swap_blocks(values):
    row, lane = iota((8, 128), 0), iota((8, 128), 1)
    turned = pltpu.roll(values, 0, 1, stride=16, stride_axis=0)
    moved = jnp.take_along_axis(turned, (lane // 16 - row + 8) % 8, axis=0, mode="promise_in_bounds")
    return jnp.take_along_axis(moved, (lane + 16 * row) % 128, axis=1, mode="promise_in_bounds")


def halves(values):
    high = values.astype(BF16)
    return high, (values - high.astype(F32)).astype(BF16)


def kernel(
    tr_h, we_h, wn_h, pm_h, df_h, dst_h, cst_h, w_h, out, bot,
    tr, we, wn, pm, df, dst, cst, w, xb, rb, vb, hx, acc, hy, hd, uh, minv, av, onehot, lhs, kc,
    inv_t, low_t, up_t, inv_b, low_b, up_b, sb, rbm,
    local_sem, ks, kr, ko, hs, hr, ys, yr, ds, dr, bs, br, bo,
):
    g, d = lax.axis_index("grp"), lax.axis_index("dev")
    me = g * DEV + d
    der = gll_derivative().astype(np.float32)

    def peer(k):
        p = lax.rem(me + k, ALL)
        return p, (lax.div(p, DEV), lax.rem(p, DEV))

    loads = [
        pltpu.make_async_copy(src, dst_ref, local_sem.at[i])
        for i, (src, dst_ref) in enumerate(
            ((df_h, df), (tr_h, tr), (we_h, we), (wn_h, wn), (pm_h, pm), (w_h, w), (dst_h, dst), (cst_h, cst))
        )
    ]
    for copy in loads:
        copy.start()

    barrier = pltpu.get_barrier_semaphore()

    def greet(k, carry):
        pl.semaphore_signal(barrier, inc=1, device_id=peer(k)[1], device_id_type=MESH)
        return carry

    lax.fori_loop(1, ALL, greet, 0)

    loads[0].wait()
    xb2, rb2 = xb.reshape(ALL * 16, 128), rb.reshape(ALL * 16, 128)

    def pack(tile, carry):
        for group in range(9):
            rows = df[pl.ds(group * 128 + tile, 8, stride=16), :]
            xb2[pl.ds(tile * 128 + group, 8, stride=16), :] = swap_blocks(rows)
        return carry

    lax.fori_loop(0, 16, pack, 0)
    own = pltpu.make_async_copy(xb.at[me, pl.ds(0, 9)], rb.at[me, pl.ds(0, 9)], ko)
    own.start()
    pl.semaphore_wait(barrier, ALL - 1)

    def send_kappa(k, carry):
        p, where = peer(k)
        pltpu.make_async_remote_copy(
            xb.at[p, pl.ds(0, 9)], rb.at[me, pl.ds(0, 9)], ks, kr, device_id=where, device_id_type=MESH
        ).start()
        return carry

    lax.fori_loop(1, ALL, send_kappa, 0)

    for copy in loads[1:]:
        copy.wait()
    for x in range(8):
        vb[0, x] = jnp.broadcast_to(pm[x : x + 1, :], (8, 128))

    def advect(block, carry):
        first = block * 8
        cells = [
            [tr[pl.ds((first + j) * 64 + x, 8, stride=8), :] for x in range(8)] for j in range(8)
        ]
        stacked = jnp.concatenate([c for level in cells for c in level], axis=0)
        product = jnp.dot(jnp.concatenate(halves(stacked), axis=1), w[...], preferred_element_type=F32)
        north = product[:, :128] + product[:, 128:]
        for j in range(8):
            for x in range(8):
                base = x // 4 * 4
                east = sum(float(der[x % 4, k]) * cells[j][base + k] for k in range(4))
                at = pl.ds((first + j) * 8 + x, 1)
                row = (j * 8 + x) * 8
                moved = cells[j][x] - (we[at, :] * east + wn[at, :] * north[row : row + 8])
                vb[1 + first + j, x] = pm[x : x + 1, :] * moved
        return carry

    row_copies = []
    for part, (lo, hi) in enumerate(CUTS):
        lax.fori_loop(3 * part, 3 * part + 3, advect, 0)
        span = pl.ds(lo, hi - lo)
        pair = []
        for side, (x, step) in enumerate(((7, 1), (0, GRP - 1))):
            copy = pltpu.make_async_remote_copy(
                vb.at[span, x], hx.at[side, span], hs.at[side, part], hr.at[side, part],
                device_id=(lax.rem(g + step, GRP), d), device_id_type=MESH,
            )
            copy.start()
            pair.append(copy)
        row_copies.append(pair)

    lane = iota((8, 128), 1)

    def gather_edges(x, carry):
        first = last = jnp.zeros((8, 128), F32)
        for s in range(LEV + 1):
            value = vb[s, x]
            first = jnp.where(lane == s, pltpu.roll(value, s, 1), first)
            last = jnp.where(lane == s, pltpu.roll(value, s + 1, 1), last)
        acc[0, x] = first
        acc[1, x] = last
        return carry

    lax.fori_loop(0, 8, gather_edges, 0)
    up_g, down_g = lax.rem(g + 1, GRP), lax.rem(g + GRP - 1, GRP)
    up_d, down_d = lax.rem(d + 1, DEV), lax.rem(d + DEV - 1, DEV)
    edge_copies = [
        pltpu.make_async_remote_copy(src, to, s, r, device_id=where, device_id_type=MESH)
        for src, to, s, r, where in (
            (acc.at[1], hy.at[0], ys.at[0], yr.at[0], (g, up_d)),
            (acc.at[0], hy.at[1], ys.at[1], yr.at[1], (g, down_d)),
            (acc.at[1, 7], hd.at[0], ds.at[0], dr.at[0], (up_g, up_d)),
            (acc.at[1, 0], hd.at[1], ds.at[1], dr.at[1], (down_g, up_d)),
            (acc.at[0, 7], hd.at[2], ds.at[2], dr.at[2], (up_g, down_d)),
            (acc.at[0, 0], hd.at[3], ds.at[3], dr.at[3], (down_g, down_d)),
        )
    ]
    for copy in edge_copies:
        copy.start()

    devices = iota((ALL, 128), 0)
    earlier = jnp.concatenate(
        [(iota((128, 128), 0) < iota((128, 128), 1)).astype(F32), jnp.ones((128, 128), F32)], axis=1
    ).astype(BF16)

    def place(x, before):
        target = jnp.broadcast_to(dst[pl.ds(x, 1), :], (ALL, 128))
        match = (target == devices).astype(F32)
        counts = jnp.dot(match.astype(BF16), earlier, preferred_element_type=F32)
        rank = jnp.sum((counts[:, :128] + before) * match, axis=0, keepdims=True)
        slot = dst[pl.ds(x, 1), :] * 16 + rank.astype(jnp.int32)
        at = pl.ds(pl.multiple_of(x * 128, 128), 128)

        def fill(block, carry):
            rows = block * 256 + iota((256, 128), 0)
            hit = (rows == jnp.broadcast_to(slot, (256, 128))).astype(F32)
            onehot[pl.ds(pl.multiple_of(block * 256, 256), 256), at] = hit.astype(BF16)
            return carry

        lax.fori_loop(0, 8, fill, 0)
        return before + counts[:, 128:]

    lax.fori_loop(0, 8, place, jnp.zeros((ALL, 128), F32))

    for copy in edge_copies:
        copy.wait()
    for side in range(2):
        uh[side, 0] = hy[side, 0] + hd[2 * side]
        uh[side, 7] = hy[side, 7] + hd[2 * side + 1]
        middle = hy[side, 3] + hy[side, 4]
        for x in (1, 2, 5, 6):
            uh[side, x] = hy[side, x]
        uh[side, 3] = middle
        uh[side, 4] = middle

    own.wait()
    sized = rb.at[pl.ds(0, ALL - 1), pl.ds(0, 9)]
    pltpu.make_async_copy(sized, sized, kr).wait()

    def unpack(tile, carry):
        at = pl.ds(pl.multiple_of(tile * 128, 128), 128)
        for group in range(9):
            values = swap_blocks(rb2[pl.ds(tile * 128 + group, 8, stride=16), :])
            rest = values - values.astype(BF16).astype(F32)
            lhs[group * 16 : group * 16 + 16, at] = jnp.concatenate([values, rest], axis=0).astype(BF16)
        return carry

    lax.fori_loop(0, 16, unpack, 0)

    def columns(x, carry):
        at = pl.ds(pl.multiple_of(x * 256, 256), 256)
        found = jnp.dot(lhs[...], onehot[:, at], preferred_element_type=F32)
        for group in range(9):
            whole = found[group * 16 : group * 16 + 8] + found[group * 16 + 8 : group * 16 + 16]
            for half in range(2):
                kc[pl.ds(group * 64 + 2 * x + half, 8, stride=8), :] = whole[:, half * 128 : half * 128 + 128]
        return carry

    lax.fori_loop(0, 4, columns, 0)

    def tile(k):
        return pl.ds(pl.multiple_of(k * 8, 8), 8)

    def eliminate(i, carry):
        gain_t, h_t, gain_b, h_b = carry
        k = i
        kk = LEV - 1 - i
        next_t = jnp.where(k < LEV - 1, 0.5 * (kc[tile(k), :] + kc[tile(jnp.minimum(k + 1, LEV - 1)), :]), 0.0)
        e = 1.0 + gain_t
        inv = 1.0 / (e + next_t)
        inv_t[tile(k), :] = inv
        low_t[tile(k), :] = h_t * inv
        up = next_t * inv
        up_t[tile(k), :] = up
        next_b = jnp.where(kk > 0, 0.5 * (kc[tile(kk), :] + kc[tile(jnp.maximum(kk - 1, 0)), :]), 0.0)
        e_b = 1.0 + gain_b
        inv2 = 1.0 / (e_b + next_b)
        inv_b[tile(kk), :] = inv2
        low_b[tile(kk), :] = h_b * inv2
        up2 = next_b * inv2
        up_b[tile(kk), :] = up2
        return up * e, next_t, up2 * e_b, next_b

    zero = jnp.zeros((8, 128), F32)
    lax.fori_loop(0, LEV, eliminate, (zero,) * 4)

    start_lane, end_lane = lane == 0, lane == 127
    at_first, at_last = lane % 4 == 0, lane % 4 == 3

    def edge_sum(s):
        u = [vb[s, x] for x in range(8)]
        u[0] = u[0] + hx[0, s]
        u[7] = u[7] + hx[1, s]
        u[3] = u[3] + u[4]
        result = [None] * 8
        for x in (0, 1, 2, 3, 5, 6, 7):
            from_left = pltpu.roll(uh[0, x], lax.rem(128 - s, 128), 1)
            from_right = pltpu.roll(uh[1, x], 127 - s, 1)
            left = jnp.where(start_lane, from_left, pltpu.roll(u[x], 1, 1))
            right = jnp.where(end_lane, from_right, pltpu.roll(u[x], 127, 1))
            result[x] = u[x] + jnp.where(at_first, left, jnp.where(at_last, right, 0.0))
        result[4] = result[3]
        return result

    for part, (lo, hi) in enumerate(CUTS):
        for copy in row_copies[part]:
            copy.wait_recv()
        if part == 0:
            for x, value in enumerate(edge_sum(jnp.int32(0))):
                minv[x] = 1.0 / value

        def average(s, carry):
            for x, value in enumerate(edge_sum(s)):
                av[pl.ds((s - 1) * 64 + x, 8, stride=8), :] = value * minv[x]
            return carry

        lax.fori_loop(max(lo, 1), hi, average, 0)

    def at_level(k, f):
        return pl.ds(pl.multiple_of(k * 64 + f * 8, 8), 8)

    def sweep_1(k, previous):
        inv, low = inv_t[tile(k), :], low_t[tile(k), :]
        current = tuple(av[at_level(k, f), :] * inv + low * previous[f] for f in range(TRC))
        for f in range(TRC):
            av[at_level(k, f), :] = current[f]
        return current

    lax.fori_loop(0, LEV, sweep_1, (zero,) * TRC)
    second, third = cst[...] >= 2, cst[...] >= 3

    def sweep_2(i, carry):
        following, previous = carry
        k = LEV - 1 - i
        up = up_t[tile(k), :]
        inv = jnp.where(second, inv_b[tile(k), :], 1.0)
        low = jnp.where(second, low_b[tile(k), :], 0.0)
        solved = tuple(av[at_level(k, f), :] + up * following[f] for f in range(TRC))
        current = tuple(solved[f] * inv + low * previous[f] for f in range(TRC))
        for f in range(TRC):
            av[at_level(k, f), :] = current[f]
        return solved, current

    lax.fori_loop(0, LEV, sweep_2, ((zero,) * TRC, (zero,) * TRC))

    def sweep_3(k, carry):
        following, previous = carry
        up = jnp.where(second, up_b[tile(k), :], 0.0)
        inv = jnp.where(third, inv_t[tile(k), :], 1.0)
        low = jnp.where(third, low_t[tile(k), :], 0.0)
        solved = tuple(av[at_level(k, f), :] + up * following[f] for f in range(TRC))
        current = tuple(solved[f] * inv + low * previous[f] for f in range(TRC))
        for f in range(TRC):
            av[at_level(k, f), :] = current[f]
        return solved, current

    lax.fori_loop(0, LEV, sweep_3, ((zero,) * TRC, (zero,) * TRC))

    last = jnp.concatenate(
        [av[pl.ds((LEV - 1) * 64 + x, 8, stride=8), :] for x in range(8)], axis=1
    )
    rest = last - last.astype(BF16).astype(F32)
    both = jnp.concatenate([last, rest], axis=0).astype(BF16)
    for block in range(8):
        spread = lax.dot_general(
            both, onehot[block * 256 : block * 256 + 256, :], (((1,), (1,)), ((), ())), preferred_element_type=F32
        )
        whole = spread[:8] + spread[8:]
        for half in range(2):
            at = (2 * block + half) * 8
            sb[at : at + 8, :] = swap_blocks(whole[:, half * 128 : half * 128 + 128])
    own_bottom = pltpu.make_async_copy(sb.at[me], rbm.at[me], bo)
    own_bottom.start()

    def send_bottom(k, carry):
        p, where = peer(k)
        pltpu.make_async_remote_copy(
            sb.at[p], rbm.at[me], bs, br, device_id=where, device_id_type=MESH
        ).start()
        return carry

    lax.fori_loop(1, ALL, send_bottom, 0)

    def sweep_4(i, following):
        k = LEV - 1 - i
        up = jnp.where(third, up_t[tile(k), :], 0.0)
        solved = tuple(av[at_level(k, f), :] + up * following[f] for f in range(TRC))
        for f in range(TRC):
            out[at_level(k, f), :] = solved[f]
        return solved

    lax.fori_loop(0, LEV, sweep_4, (zero,) * TRC)

    own_bottom.wait()
    sized = rbm.at[pl.ds(0, ALL - 1)]
    pltpu.make_async_copy(sized, sized, br).wait()
    for t in range(16):
        bot[pl.ds(t, 8, stride=16), :] = swap_blocks(rbm[t * 8 : t * 8 + 8, :])

    for pair in row_copies:
        for copy in pair:
            copy.wait_send()
    sized = xb.at[pl.ds(0, ALL - 1), pl.ds(0, 9)]
    pltpu.make_async_copy(sized, sized, ks).wait()
    sized = sb.at[pl.ds(0, ALL - 1)]
    pltpu.make_async_copy(sized, sized, bs).wait()


def shards(tracers, wind_east, wind_north, point_mass, diffusivity, destination, column_cost):
    weights = jnp.asarray(north_weights())
    vmem = pltpu.VMEM
    dma = pltpu.SemaphoreType.DMA
    mixed, bottoms = pl.pallas_call(
        kernel,
        out_shape=[jax.ShapeDtypeStruct((ROWS, 128), F32), jax.ShapeDtypeStruct((128, 128), F32)],
        in_specs=[pl.BlockSpec(memory_space=pl.ANY)] * 8,
        out_specs=[pl.BlockSpec(memory_space=vmem)] * 2,
        scratch_shapes=[
            vmem((ROWS, 128), F32),
            vmem((LEV * 8, 128), F32),
            vmem((LEV * 8, 128), F32),
            vmem((8, 128), F32),
            vmem((LEV * 16, 128), F32),
            vmem((8, 128), jnp.int32),
            vmem((8, 128), jnp.int32),
            vmem((256, 256), BF16),
            vmem((ALL, 16, 128), F32),
            vmem((ALL, 16, 128), F32),
            vmem((LEV + 1, 8, 8, 128), F32),
            vmem((2, LEV + 1, 8, 128), F32),
            vmem((2, 8, 8, 128), F32),
            vmem((2, 8, 8, 128), F32),
            vmem((4, 8, 128), F32),
            vmem((2, 8, 8, 128), F32),
            vmem((8, 8, 128), F32),
            vmem((ROWS, 128), F32),
            vmem((ALL * 16, 1024), BF16),
            vmem((LEV * 2, ALL * 16), BF16),
            vmem((LEV * 8, 128), F32),
        ]
        + [vmem((LEV * 8, 128), F32)] * 6
        + [vmem((128, 128), F32)] * 2
        + [dma((8,)), dma, dma, dma, dma((2, 3)), dma((2, 3)), dma((2,)), dma((2,)), dma((4,)), dma((4,)), dma, dma, dma],
        compiler_params=pltpu.CompilerParams(
            collective_id=0, has_side_effects=True, vmem_limit_bytes=48 * 2**20
        ),
        cost_estimate=pl.CostEstimate(flops=2 * 10**9, bytes_accessed=7 * 10**6, transcendentals=0),
        name="tracer_step",
    )(
        tracers.reshape(ROWS, 128),
        wind_east.reshape(LEV * 8, 128),
        wind_north.reshape(LEV * 8, 128),
        point_mass,
        diffusivity.reshape(LEV * 16, 128),
        destination.reshape(8, 128),
        column_cost.reshape(8, 128),
        weights,
    )
    return mixed.reshape(LEV, TRC, 8, 128), bottoms.reshape(TRC, 1, ALL * 16)


def solution(mesh):
    return jax.shard_map(
        shards,
        mesh=mesh,
        in_specs=(
            P(None, None, "grp", "dev"),
            P(None, "grp", "dev"),
            P(None, "grp", "dev"),
            P("grp", "dev"),
            P(None, ("grp", "dev"), None),
            P(("grp", "dev"), None, None),
            P(("grp", "dev"), None),
        ),
        out_specs=(P(None, None, "grp", "dev"), P(None, ("grp", "dev"), None)),
        check_vma=False,
    )
```

```python
import jax
import jax.numpy as jnp
import numpy as np
from jax import lax
from jax.experimental import pallas as pl
from jax.experimental.pallas import tpu as pltpu
from jax.sharding import PartitionSpec as P

LEV = 72
TRC = 8
ROWS = LEV * TRC * 8
GRP = 4
DEV = 32
ALL = GRP * DEV
CUTS = ((0, 25), (25, 49), (49, 73))
MESH = pl.DeviceIdType.MESH
F32 = jnp.float32
BF16 = jnp.bfloat16


def gll_derivative():
    points = np.array([-1.0, -1.0 / np.sqrt(5.0), 1.0 / np.sqrt(5.0), 1.0])
    der = np.zeros((4, 4))
    for i in range(4):
        for k in range(4):
            others = [m for m in range(4) if m != k]
            if i == k:
                der[i, k] = sum(1.0 / (points[k] - points[m]) for m in others)
            else:
                term = 1.0
                for m in others:
                    if m != i:
                        term *= (points[i] - points[m]) / (points[k] - points[m])
                der[i, k] = term / (points[k] - points[i])
    return der


def north_weights():
    along = np.kron(np.eye(32), gll_derivative().T).astype(np.float32)
    high = along.astype(jnp.bfloat16)
    low = (along - high.astype(np.float32)).astype(jnp.bfloat16)
    return np.block([[high, low], [high, np.zeros_like(low)]])


def iota(shape, dim):
    return lax.broadcasted_iota(jnp.int32, shape, dim)


def swap_blocks(values):
    row, lane = iota((8, 128), 0), iota((8, 128), 1)
    turned = pltpu.roll(values, 0, 1, stride=16, stride_axis=0)
    moved = jnp.take_along_axis(turned, (lane // 16 - row + 8) % 8, axis=0, mode="promise_in_bounds")
    return jnp.take_along_axis(moved, (lane + 16 * row) % 128, axis=1, mode="promise_in_bounds")


def halves(values):
    high = values.astype(BF16)
    return high, (values - high.astype(F32)).astype(BF16)


def kernel(
    tr_h, we_h, wn_h, pm_h, df_h, dst_h, cst_h, w_h, out, bot,
    tr, we, wn, pm, df, dst, cst, w, xb, rb, vb, hx, acc, hy, hd, uh, minv, av, onehot, lhs, kc,
    inv_t, low_t, up_t, inv_b, low_b, up_b, sb, rbm,
    local_sem, ks, kr, ko, hs, hr, ys, yr, ds, dr, bs, br, bo,
):
    g, d = lax.axis_index("grp"), lax.axis_index("dev")
    me = g * DEV + d
    der = gll_derivative().astype(np.float32)

    def peer(k):
        p = lax.rem(me + k, ALL)
        return p, (lax.div(p, DEV), lax.rem(p, DEV))

    loads = [
        pltpu.make_async_copy(src, dst_ref, local_sem.at[i])
        for i, (src, dst_ref) in enumerate(
            ((df_h, df), (tr_h, tr), (we_h, we), (wn_h, wn), (pm_h, pm), (w_h, w), (dst_h, dst), (cst_h, cst))
        )
    ]
    for copy in loads:
        copy.start()

    barrier = pltpu.get_barrier_semaphore()

    def greet(k, carry):
        pl.semaphore_signal(barrier, inc=1, device_id=peer(k)[1], device_id_type=MESH)
        return carry

    lax.fori_loop(1, ALL, greet, 0)

    loads[0].wait()
    xb2, rb2 = xb.reshape(ALL * 16, 128), rb.reshape(ALL * 16, 128)

    def pack(tile, carry):
        for group in range(9):
            rows = df[pl.ds(group * 128 + tile, 8, stride=16), :]
            xb2[pl.ds(tile * 128 + group, 8, stride=16), :] = swap_blocks(rows)
        return carry

    lax.fori_loop(0, 16, pack, 0, unroll=2)
    own = pltpu.make_async_copy(xb.at[me, pl.ds(0, 9)], rb.at[me, pl.ds(0, 9)], ko)
    own.start()
    pl.semaphore_wait(barrier, ALL - 1)

    def send_kappa(k, carry):
        p, where = peer(k)
        pltpu.make_async_remote_copy(
            xb.at[p, pl.ds(0, 9)], rb.at[me, pl.ds(0, 9)], ks, kr, device_id=where, device_id_type=MESH
        ).start()
        return carry

    lax.fori_loop(1, ALL, send_kappa, 0)

    for copy in loads[1:]:
        copy.wait()
    for x in range(8):
        vb[0, x] = jnp.broadcast_to(pm[x : x + 1, :], (8, 128))

    def advect(block, carry):
        first = block * 8
        cells = [
            [tr[pl.ds((first + j) * 64 + x, 8, stride=8), :] for x in range(8)] for j in range(8)
        ]
        stacked = jnp.concatenate([c for level in cells for c in level], axis=0)
        product = jnp.dot(jnp.concatenate(halves(stacked), axis=1), w[...], preferred_element_type=F32)
        north = product[:, :128] + product[:, 128:]
        for j in range(8):
            for x in range(8):
                base = x // 4 * 4
                east = sum(float(der[x % 4, k]) * cells[j][base + k] for k in range(4))
                at = pl.ds((first + j) * 8 + x, 1)
                row = (j * 8 + x) * 8
                moved = cells[j][x] - (we[at, :] * east + wn[at, :] * north[row : row + 8])
                vb[1 + first + j, x] = pm[x : x + 1, :] * moved
        return carry

    row_copies = []
    for part, (lo, hi) in enumerate(CUTS):
        lax.fori_loop(3 * part, 3 * part + 3, advect, 0)
        span = pl.ds(lo, hi - lo)
        pair = []
        for side, (x, step) in enumerate(((7, 1), (0, GRP - 1))):
            copy = pltpu.make_async_remote_copy(
                vb.at[span, x], hx.at[side, span], hs.at[side, part], hr.at[side, part],
                device_id=(lax.rem(g + step, GRP), d), device_id_type=MESH,
            )
            copy.start()
            pair.append(copy)
        row_copies.append(pair)

    lane = iota((8, 128), 1)

    def gather_edges(x, carry):
        first = last = jnp.zeros((8, 128), F32)
        for s in range(LEV + 1):
            value = vb[s, x]
            first = jnp.where(lane == s, pltpu.roll(value, s, 1), first)
            last = jnp.where(lane == s, pltpu.roll(value, s + 1, 1), last)
        acc[0, x] = first
        acc[1, x] = last
        return carry

    lax.fori_loop(0, 8, gather_edges, 0)
    up_g, down_g = lax.rem(g + 1, GRP), lax.rem(g + GRP - 1, GRP)
    up_d, down_d = lax.rem(d + 1, DEV), lax.rem(d + DEV - 1, DEV)
    edge_copies = [
        pltpu.make_async_remote_copy(src, to, s, r, device_id=where, device_id_type=MESH)
        for src, to, s, r, where in (
            (acc.at[1], hy.at[0], ys.at[0], yr.at[0], (g, up_d)),
            (acc.at[0], hy.at[1], ys.at[1], yr.at[1], (g, down_d)),
            (acc.at[1, 7], hd.at[0], ds.at[0], dr.at[0], (up_g, up_d)),
            (acc.at[1, 0], hd.at[1], ds.at[1], dr.at[1], (down_g, up_d)),
            (acc.at[0, 7], hd.at[2], ds.at[2], dr.at[2], (up_g, down_d)),
            (acc.at[0, 0], hd.at[3], ds.at[3], dr.at[3], (down_g, down_d)),
        )
    ]
    for copy in edge_copies:
        copy.start()

    devices = iota((ALL, 128), 0)
    earlier = jnp.concatenate(
        [(iota((128, 128), 0) < iota((128, 128), 1)).astype(F32), jnp.ones((128, 128), F32)], axis=1
    ).astype(BF16)

    def place(x, before):
        target = jnp.broadcast_to(dst[pl.ds(x, 1), :], (ALL, 128))
        match = (target == devices).astype(F32)
        counts = jnp.dot(match.astype(BF16), earlier, preferred_element_type=F32)
        rank = jnp.sum((counts[:, :128] + before) * match, axis=0, keepdims=True)
        slot = dst[pl.ds(x, 1), :] * 16 + rank.astype(jnp.int32)
        at = pl.ds(pl.multiple_of(x * 128, 128), 128)

        def fill(block, carry):
            rows = block * 256 + iota((256, 128), 0)
            hit = (rows == jnp.broadcast_to(slot, (256, 128))).astype(F32)
            onehot[pl.ds(pl.multiple_of(block * 256, 256), 256), at] = hit.astype(BF16)
            return carry

        lax.fori_loop(0, 8, fill, 0)
        return before + counts[:, 128:]

    lax.fori_loop(0, 8, place, jnp.zeros((ALL, 128), F32))

    for copy in edge_copies:
        copy.wait()
    for side in range(2):
        uh[side, 0] = hy[side, 0] + hd[2 * side]
        uh[side, 7] = hy[side, 7] + hd[2 * side + 1]
        middle = hy[side, 3] + hy[side, 4]
        for x in (1, 2, 5, 6):
            uh[side, x] = hy[side, x]
        uh[side, 3] = middle
        uh[side, 4] = middle

    start_lane, end_lane = lane == 0, lane == 127
    at_first, at_last = lane % 4 == 0, lane % 4 == 3

    def across(s, x, u):
        from_left = pltpu.roll(uh[0, x], lax.rem(128 - s, 128), 1)
        from_right = pltpu.roll(uh[1, x], 127 - s, 1)
        left = jnp.where(start_lane, from_left, pltpu.roll(u, 1, 1))
        right = jnp.where(end_lane, from_right, pltpu.roll(u, 127, 1))
        return u + jnp.where(at_first, left, jnp.where(at_last, right, 0.0))

    def inner_sum(s):
        middle = across(s, 3, vb[s, 3] + vb[s, 4])
        return [(3, middle), (4, middle)] + [(x, across(s, x, vb[s, x])) for x in (1, 2, 5, 6)]

    def outer_sum(s):
        return [(x, across(s, x, vb[s, x] + hx[side, s])) for side, x in ((0, 0), (1, 7))]

    for x, value in inner_sum(jnp.int32(0)):
        minv[x] = 1.0 / value

    def average_inner(s, carry):
        for x, value in inner_sum(s):
            av[pl.ds((s - 1) * 64 + x, 8, stride=8), :] = value * minv[x]
        return carry

    lax.fori_loop(1, LEV + 1, average_inner, 0, unroll=4)

    own.wait()
    sized = rb.at[pl.ds(0, ALL - 1), pl.ds(0, 9)]
    pltpu.make_async_copy(sized, sized, kr).wait()

    def unpack(tile, carry):
        at = pl.ds(pl.multiple_of(tile * 128, 128), 128)
        for group in range(9):
            values = swap_blocks(rb2[pl.ds(tile * 128 + group, 8, stride=16), :])
            rest = values - values.astype(BF16).astype(F32)
            lhs[group * 16 : group * 16 + 16, at] = jnp.concatenate([values, rest], axis=0).astype(BF16)
        return carry

    lax.fori_loop(0, 16, unpack, 0, unroll=2)

    def columns(x, carry):
        at = pl.ds(pl.multiple_of(x * 256, 256), 256)
        found = jnp.dot(lhs[...], onehot[:, at], preferred_element_type=F32)
        for group in range(9):
            whole = found[group * 16 : group * 16 + 8] + found[group * 16 + 8 : group * 16 + 16]
            for half in range(2):
                kc[pl.ds(group * 64 + 2 * x + half, 8, stride=8), :] = whole[:, half * 128 : half * 128 + 128]
        return carry

    lax.fori_loop(0, 4, columns, 0)

    def tile(k):
        return pl.ds(pl.multiple_of(k * 8, 8), 8)

    def eliminate(i, carry):
        gain_t, h_t, gain_b, h_b = carry
        k = i
        kk = LEV - 1 - i
        next_t = jnp.where(k < LEV - 1, 0.5 * (kc[tile(k), :] + kc[tile(jnp.minimum(k + 1, LEV - 1)), :]), 0.0)
        e = 1.0 + gain_t
        inv = 1.0 / (e + next_t)
        inv_t[tile(k), :] = inv
        low_t[tile(k), :] = h_t * inv
        up = next_t * inv
        up_t[tile(k), :] = up
        next_b = jnp.where(kk > 0, 0.5 * (kc[tile(kk), :] + kc[tile(jnp.maximum(kk - 1, 0)), :]), 0.0)
        e_b = 1.0 + gain_b
        inv2 = 1.0 / (e_b + next_b)
        inv_b[tile(kk), :] = inv2
        low_b[tile(kk), :] = h_b * inv2
        up2 = next_b * inv2
        up_b[tile(kk), :] = up2
        return up * e, next_t, up2 * e_b, next_b

    zero = jnp.zeros((8, 128), F32)
    lax.fori_loop(0, LEV, eliminate, (zero,) * 4, unroll=4)

    for part, (lo, hi) in enumerate(CUTS):
        for copy in row_copies[part]:
            copy.wait_recv()
        if part == 0:
            for x, value in outer_sum(jnp.int32(0)):
                minv[x] = 1.0 / value

        def average_outer(s, carry):
            for x, value in outer_sum(s):
                av[pl.ds((s - 1) * 64 + x, 8, stride=8), :] = value * minv[x]
            return carry

        lax.fori_loop(max(lo, 1), hi, average_outer, 0, unroll=4)

    def at_level(k, f):
        return pl.ds(pl.multiple_of(k * 64 + f * 8, 8), 8)

    def sweep_1(k, previous):
        inv, low = inv_t[tile(k), :], low_t[tile(k), :]
        current = tuple(av[at_level(k, f), :] * inv + low * previous[f] for f in range(TRC))
        for f in range(TRC):
            av[at_level(k, f), :] = current[f]
        return current

    lax.fori_loop(0, LEV, sweep_1, (zero,) * TRC, unroll=4)
    second, third = cst[...] >= 2, cst[...] >= 3

    def sweep_2(i, carry):
        following, previous = carry
        k = LEV - 1 - i
        up = up_t[tile(k), :]
        inv = jnp.where(second, inv_b[tile(k), :], 1.0)
        low = jnp.where(second, low_b[tile(k), :], 0.0)
        solved = tuple(av[at_level(k, f), :] + up * following[f] for f in range(TRC))
        current = tuple(solved[f] * inv + low * previous[f] for f in range(TRC))
        for f in range(TRC):
            av[at_level(k, f), :] = current[f]
        return solved, current

    lax.fori_loop(0, LEV, sweep_2, ((zero,) * TRC, (zero,) * TRC), unroll=4)

    def sweep_3(k, carry):
        following, previous = carry
        up = jnp.where(second, up_b[tile(k), :], 0.0)
        inv = jnp.where(third, inv_t[tile(k), :], 1.0)
        low = jnp.where(third, low_t[tile(k), :], 0.0)
        solved = tuple(av[at_level(k, f), :] + up * following[f] for f in range(TRC))
        current = tuple(solved[f] * inv + low * previous[f] for f in range(TRC))
        for f in range(TRC):
            av[at_level(k, f), :] = current[f]
        return solved, current

    lax.fori_loop(0, LEV, sweep_3, ((zero,) * TRC, (zero,) * TRC), unroll=4)

    last = jnp.concatenate(
        [av[pl.ds((LEV - 1) * 64 + x, 8, stride=8), :] for x in range(8)], axis=1
    )
    rest = last - last.astype(BF16).astype(F32)
    both = jnp.concatenate([last, rest], axis=0).astype(BF16)
    for block in range(8):
        spread = lax.dot_general(
            both, onehot[block * 256 : block * 256 + 256, :], (((1,), (1,)), ((), ())), preferred_element_type=F32
        )
        whole = spread[:8] + spread[8:]
        for half in range(2):
            at = (2 * block + half) * 8
            sb[at : at + 8, :] = swap_blocks(whole[:, half * 128 : half * 128 + 128])
    own_bottom = pltpu.make_async_copy(sb.at[me], rbm.at[me], bo)
    own_bottom.start()

    def send_bottom(k, carry):
        p, where = peer(k)
        pltpu.make_async_remote_copy(
            sb.at[p], rbm.at[me], bs, br, device_id=where, device_id_type=MESH
        ).start()
        return carry

    lax.fori_loop(1, ALL, send_bottom, 0)

    def sweep_4(i, following):
        k = LEV - 1 - i
        up = jnp.where(third, up_t[tile(k), :], 0.0)
        solved = tuple(av[at_level(k, f), :] + up * following[f] for f in range(TRC))
        for f in range(TRC):
            out[at_level(k, f), :] = solved[f]
        return solved

    lax.fori_loop(0, LEV, sweep_4, (zero,) * TRC, unroll=4)

    own_bottom.wait()
    sized = rbm.at[pl.ds(0, ALL - 1)]
    pltpu.make_async_copy(sized, sized, br).wait()
    for t in range(16):
        bot[pl.ds(t, 8, stride=16), :] = swap_blocks(rbm[t * 8 : t * 8 + 8, :])

    for pair in row_copies:
        for copy in pair:
            copy.wait_send()
    sized = xb.at[pl.ds(0, ALL - 1), pl.ds(0, 9)]
    pltpu.make_async_copy(sized, sized, ks).wait()
    sized = sb.at[pl.ds(0, ALL - 1)]
    pltpu.make_async_copy(sized, sized, bs).wait()


def shards(tracers, wind_east, wind_north, point_mass, diffusivity, destination, column_cost):
    weights = jnp.asarray(north_weights())
    vmem = pltpu.VMEM
    dma = pltpu.SemaphoreType.DMA
    mixed, bottoms = pl.pallas_call(
        kernel,
        out_shape=[jax.ShapeDtypeStruct((ROWS, 128), F32), jax.ShapeDtypeStruct((128, 128), F32)],
        in_specs=[pl.BlockSpec(memory_space=pltpu.HBM)] * 8,
        out_specs=[pl.BlockSpec(memory_space=vmem)] * 2,
        scratch_shapes=[
            vmem((ROWS, 128), F32),
            vmem((LEV * 8, 128), F32),
            vmem((LEV * 8, 128), F32),
            vmem((8, 128), F32),
            vmem((LEV * 16, 128), F32),
            vmem((8, 128), jnp.int32),
            vmem((8, 128), jnp.int32),
            vmem((256, 256), BF16),
            vmem((ALL, 16, 128), F32),
            vmem((ALL, 16, 128), F32),
            vmem((LEV + 1, 8, 8, 128), F32),
            vmem((2, LEV + 1, 8, 128), F32),
            vmem((2, 8, 8, 128), F32),
            vmem((2, 8, 8, 128), F32),
            vmem((4, 8, 128), F32),
            vmem((2, 8, 8, 128), F32),
            vmem((8, 8, 128), F32),
            vmem((ROWS, 128), F32),
            vmem((ALL * 16, 1024), BF16),
            vmem((LEV * 2, ALL * 16), BF16),
            vmem((LEV * 8, 128), F32),
        ]
        + [vmem((LEV * 8, 128), F32)] * 6
        + [vmem((128, 128), F32)] * 2
        + [dma((8,)), dma, dma, dma, dma((2, 3)), dma((2, 3)), dma((2,)), dma((2,)), dma((4,)), dma((4,)), dma, dma, dma],
        compiler_params=pltpu.CompilerParams(
            collective_id=0, has_side_effects=True, vmem_limit_bytes=63 * 2**20
        ),
        cost_estimate=pl.CostEstimate(flops=2 * 10**9, bytes_accessed=7 * 10**6, transcendentals=0),
        name="tracer_step",
    )(
        tracers.reshape(ROWS, 128),
        wind_east.reshape(LEV * 8, 128),
        wind_north.reshape(LEV * 8, 128),
        point_mass,
        diffusivity.reshape(LEV * 16, 128),
        destination.reshape(8, 128),
        column_cost.reshape(8, 128),
        weights,
    )
    return mixed.reshape(LEV, TRC, 8, 128), bottoms.reshape(TRC, 1, ALL * 16)


def solution(mesh):
    return jax.shard_map(
        shards,
        mesh=mesh,
        in_specs=(
            P(None, None, "grp", "dev"),
            P(None, "grp", "dev"),
            P(None, "grp", "dev"),
            P("grp", "dev"),
            P(None, ("grp", "dev"), None),
            P(("grp", "dev"), None, None),
            P(("grp", "dev"), None),
        ),
        out_specs=(P(None, None, "grp", "dev"), P(None, ("grp", "dev"), None)),
        check_vma=False,
    )
```

```python
import jax
import jax.numpy as jnp
import numpy as np
from jax import lax
from jax.experimental import pallas as pl
from jax.experimental.pallas import tpu as pltpu
from jax.sharding import PartitionSpec as P

LEV = 72
TRC = 8
ROWS = LEV * TRC * 8
GRP = 4
DEV = 32
ALL = GRP * DEV
CUTS = ((0, 25), (25, 49), (49, 73))
MESH = pl.DeviceIdType.MESH
F32 = jnp.float32
BF16 = jnp.bfloat16


def gll_derivative():
    points = np.array([-1.0, -1.0 / np.sqrt(5.0), 1.0 / np.sqrt(5.0), 1.0])
    der = np.zeros((4, 4))
    for i in range(4):
        for k in range(4):
            others = [m for m in range(4) if m != k]
            if i == k:
                der[i, k] = sum(1.0 / (points[k] - points[m]) for m in others)
            else:
                term = 1.0
                for m in others:
                    if m != i:
                        term *= (points[i] - points[m]) / (points[k] - points[m])
                der[i, k] = term / (points[k] - points[i])
    return der


def north_weights():
    along = np.kron(np.eye(32), gll_derivative().T).astype(np.float32)
    high = along.astype(jnp.bfloat16)
    low = (along - high.astype(np.float32)).astype(jnp.bfloat16)
    return np.block([[high, low], [high, np.zeros_like(low)]])


def iota(shape, dim):
    return lax.broadcasted_iota(jnp.int32, shape, dim)


def swap_blocks(values, last=False):
    row, lane = iota((8, 128), 0), iota((8, 128), 1)
    turned = pltpu.roll(values, 0, 1, stride=16, stride_axis=0)
    moved = jnp.take_along_axis(turned, (lane // 16 - row + 8) % 8, axis=0, mode="promise_in_bounds")
    source = lane % 8 * 16 + lane // 8 if last else lane
    return jnp.take_along_axis(moved, (source + 16 * row) % 128, axis=1, mode="promise_in_bounds")


def halves(values):
    high = values.astype(BF16)
    return high, (values - high.astype(F32)).astype(BF16)


def kernel(
    tr_h, we_h, wn_h, pm_h, df_h, dst_h, cst_h, w_h, out, rbm,
    tr, we, wn, pm, df, dst, cst, w, xb, rb, vb, hx, acc, hy, hd, uh, minv, av, rank, chosen_by, lhs, spread, kc,
    inv_t, low_t, up_t, inv_b, low_b, up_b, sb,
    local_sem, ks, kr, ko, hs, hr, ys, yr, ds, dr, bs, br, bo,
):
    g, d = lax.axis_index("grp"), lax.axis_index("dev")
    me = g * DEV + d
    der = gll_derivative().astype(np.float32)

    z, y, core = lax.div(d, 8), lax.rem(lax.div(d, 2), 4), lax.rem(d, 2)

    def eight(step, t, act, count=8):
        to_g, to_z = lax.rem(g + step, GRP), lax.rem(z + t + 1, 4)
        for i in range(count):
            to_d = to_z * 8 + lax.rem(y + i // 2 + 1, 4) * 2 + lax.rem(core + i + 1, 2)
            act(to_g * DEV + to_d, (to_g, to_d))

    def for_peers(act, beside=None):
        for turn, step in enumerate((2, 1, 3, 0)):

            def some(t, carry):
                eight(step, t, act)
                if beside is not None:
                    beside(4 * turn + t)
                return carry

            lax.fori_loop(0, 3 if step == 0 else 4, some, 0)
        eight(0, 3, act, 7)
        if beside is not None:
            beside(15)

    loads = [
        pltpu.make_async_copy(src, dst_ref, local_sem.at[i])
        for i, (src, dst_ref) in enumerate(
            ((df_h, df), (tr_h, tr), (we_h, we), (wn_h, wn), (pm_h, pm), (w_h, w), (dst_h, dst), (cst_h, cst))
        )
    ]
    for copy in loads:
        copy.start()

    barrier = pltpu.get_barrier_semaphore()

    def greet(p, where):
        pl.semaphore_signal(barrier, inc=1, device_id=where, device_id_type=MESH)

    loads[0].wait()
    xb2, rb2 = xb.reshape(ALL * 16, 128), rb.reshape(ALL * 16, 128)

    def pack(tile):
        for group in range(9):
            rows = df[pl.ds(group * 128 + tile, 8, stride=16), :]
            xb2[pl.ds(tile * 128 + group, 8, stride=16), :] = swap_blocks(rows, last=True)

    for_peers(greet, pack)
    own = pltpu.make_async_copy(xb.at[me, pl.ds(0, 9)], rb.at[me, pl.ds(0, 9)], ko)
    own.start()

    for copy in loads[1:]:
        copy.wait()
    for x in range(8):
        vb[0, x] = jnp.broadcast_to(pm[x : x + 1, :], (8, 128))

    def advect(block, carry):
        first = block * 8
        cells = [
            [tr[pl.ds((first + j) * 64 + x, 8, stride=8), :] for x in range(8)] for j in range(8)
        ]
        stacked = jnp.concatenate([c for level in cells for c in level], axis=0)
        product = jnp.dot(jnp.concatenate(halves(stacked), axis=1), w[...], preferred_element_type=F32)
        north = product[:, :128] + product[:, 128:]
        for j in range(8):
            for x in range(8):
                base = x // 4 * 4
                east = sum(float(der[x % 4, k]) * cells[j][base + k] for k in range(4))
                at = pl.ds((first + j) * 8 + x, 1)
                row = (j * 8 + x) * 8
                moved = cells[j][x] - (we[at, :] * east + wn[at, :] * north[row : row + 8])
                vb[1 + first + j, x] = pm[x : x + 1, :] * moved
        return carry

    lax.fori_loop(0, 9, advect, 0)

    lane = iota((8, 128), 1)

    def gather_edges(x, carry):
        first = last = jnp.zeros((8, 128), F32)
        for s in range(LEV + 1):
            value = pltpu.roll(vb[s, x], s + 1, 1)
            first = jnp.where(lane == s + 1, value, first)
            last = jnp.where(lane == s, value, last)
        acc[0, x] = first
        acc[1, x] = last
        return carry

    lax.fori_loop(0, 8, gather_edges, 0)
    up_g, down_g = lax.rem(g + 1, GRP), lax.rem(g + GRP - 1, GRP)
    up_d, down_d = lax.rem(d + 1, DEV), lax.rem(d + DEV - 1, DEV)
    edge_copies = [
        pltpu.make_async_remote_copy(src, to, s, r, device_id=where, device_id_type=MESH)
        for src, to, s, r, where in (
            (acc.at[1], hy.at[0], ys.at[0], yr.at[0], (g, up_d)),
            (acc.at[0], hy.at[1], ys.at[1], yr.at[1], (g, down_d)),
            (acc.at[1, 7], hd.at[0], ds.at[0], dr.at[0], (up_g, up_d)),
            (acc.at[1, 0], hd.at[1], ds.at[1], dr.at[1], (down_g, up_d)),
            (acc.at[0, 7], hd.at[2], ds.at[2], dr.at[2], (up_g, down_d)),
            (acc.at[0, 0], hd.at[3], ds.at[3], dr.at[3], (down_g, down_d)),
        )
    ]
    pl.semaphore_wait(barrier, ALL - 1)
    for copy in edge_copies:
        copy.start()

    def send_kappa(p, where):
        pltpu.make_async_remote_copy(
            xb.at[p, pl.ds(0, 9)], rb.at[me, pl.ds(0, 9)], ks, kr, device_id=where, device_id_type=MESH
        ).start()

    for_peers(send_kappa)
    row_copies = [
        [
            pltpu.make_async_remote_copy(
                vb.at[pl.ds(lo, hi - lo), x], hx.at[side, pl.ds(lo, hi - lo)], hs.at[side, part], hr.at[side, part],
                device_id=(to_g, d), device_id_type=MESH,
            )
            for side, (x, to_g) in enumerate(((7, up_g), (0, down_g)))
        ]
        for part, (lo, hi) in enumerate(CUTS)
    ]
    for pair in row_copies:
        for copy in pair:
            copy.start()

    devices = iota((ALL, 128), 0)
    earlier = jnp.concatenate(
        [(iota((128, 128), 0) < iota((128, 128), 1)).astype(F32), jnp.ones((128, 128), F32)], axis=1
    ).astype(BF16)
    before = jnp.zeros((ALL, 128), F32)
    for x in range(8):
        match = (jnp.broadcast_to(dst[x : x + 1, :], (ALL, 128)) == devices).astype(F32)
        chosen = match.astype(BF16)
        counts = jnp.dot(chosen, earlier, preferred_element_type=F32)
        order = jnp.sum((counts[:, :128] + before) * match, axis=0, keepdims=True)
        rank[x : x + 1, :] = order.astype(jnp.int32)
        at = slice(x * 128, x * 128 + 128)
        chosen_by[:ALL, at] = chosen
        chosen_by[ALL:, at] = chosen
        before = before + counts[:, 128:]

    for copy in edge_copies:
        copy.wait()
    sides = []
    for side in range(2):
        middle = hy[side, 3] + hy[side, 4]
        rows = [hy[side, x] for x in range(8)]
        rows[0] = rows[0] + hd[2 * side]
        rows[7] = rows[7] + hd[2 * side + 1]
        rows[3] = rows[4] = middle
        sides.append(rows)
    even = lane % 2 == 0
    for x in range(8):
        from_left, from_right = sides[0][x], pltpu.roll(sides[1][x], 126, 1)
        uh[0, x] = jnp.where(even, from_left, from_right)
        uh[1, x] = jnp.where(even, from_right, from_left)

    at_first, at_last = lane % 4 == 0, lane % 4 == 3
    at_end, at_side = (lane == 0) | (lane == 127), at_first | at_last

    def across(s, x, u):
        halo = pltpu.roll(uh[lax.rem(s, 2), x], lax.rem(128 - s, 128), 1)
        beside = jnp.where(at_first, pltpu.roll(u, 1, 1), pltpu.roll(u, 127, 1))
        return u + jnp.where(at_side, jnp.where(at_end, halo, beside), 0.0)

    def inner_sum(s):
        middle = across(s, 3, vb[s, 3] + vb[s, 4])
        return [(3, middle), (4, middle)] + [(x, across(s, x, vb[s, x])) for x in (1, 2, 5, 6)]

    def outer_sum(s):
        return [(x, across(s, x, vb[s, x] + hx[side, s])) for side, x in ((0, 0), (1, 7))]

    for x, value in inner_sum(jnp.int32(0)):
        minv[x] = 1.0 / value

    def average_inner(s, carry):
        for x, value in inner_sum(s):
            av[pl.ds((s - 1) * 64 + x, 8, stride=8), :] = value * minv[x]
        return carry

    lax.fori_loop(1, LEV + 1, average_inner, 0, unroll=4)

    own.wait()
    sized = rb.at[pl.ds(0, ALL - 1), pl.ds(0, 9)]
    pltpu.make_async_copy(sized, sized, kr).wait()

    for group in range(9):
        values = rb2[pl.ds(group, ALL, stride=16), :].T
        lhs[group * 128 : group * 128 + 128, :] = jnp.concatenate(halves(values), axis=1)

    def columns(pair, carry):
        at = pl.ds(pl.multiple_of(pair * 256, 256), 256)
        found = jnp.dot(lhs[...], chosen_by[:, at], preferred_element_type=F32)
        for half in range(2):
            x = 2 * pair + half
            order = jnp.broadcast_to(rank[pl.ds(x, 1), :], (8, 128))
            hits = [order == r for r in range(16)]
            for group in range(9):
                value = found[group * 128 : group * 128 + 8, half * 128 : half * 128 + 128]
                for r in range(1, 16):
                    row = group * 128 + r * 8
                    value = jnp.where(hits[r], found[row : row + 8, half * 128 : half * 128 + 128], value)
                kc[pl.ds(group * 64 + x, 8, stride=8), :] = value
        return carry

    lax.fori_loop(0, 4, columns, 0)

    def tile(k):
        return pl.ds(pl.multiple_of(k * 8, 8), 8)

    def eliminate(i, carry):
        gain_t, h_t, gain_b, h_b = carry
        k = i
        kk = LEV - 1 - i
        next_t = jnp.where(k < LEV - 1, 0.5 * (kc[tile(k), :] + kc[tile(jnp.minimum(k + 1, LEV - 1)), :]), 0.0)
        e = 1.0 + gain_t
        inv = 1.0 / (e + next_t)
        inv_t[tile(k), :] = inv
        low_t[tile(k), :] = h_t * inv
        up = next_t * inv
        up_t[tile(k), :] = up
        next_b = jnp.where(kk > 0, 0.5 * (kc[tile(kk), :] + kc[tile(jnp.maximum(kk - 1, 0)), :]), 0.0)
        e_b = 1.0 + gain_b
        inv2 = 1.0 / (e_b + next_b)
        inv_b[tile(kk), :] = inv2
        low_b[tile(kk), :] = h_b * inv2
        up2 = next_b * inv2
        up_b[tile(kk), :] = up2
        return up * e, next_t, up2 * e_b, next_b

    zero = jnp.zeros((8, 128), F32)
    carry = (zero,) * 4
    for part, (lo, hi) in enumerate(CUTS):
        for copy in row_copies[part]:
            copy.wait_recv()
        if part == 0:
            for x, value in outer_sum(jnp.int32(0)):
                minv[x] = 1.0 / value

        def both(s, carry):
            for x, value in outer_sum(s):
                av[pl.ds((s - 1) * 64 + x, 8, stride=8), :] = value * minv[x]
            return eliminate(s - 1, carry)

        carry = lax.fori_loop(max(lo, 1), hi, both, carry, unroll=4)

    def at_level(k, f):
        return pl.ds(pl.multiple_of(k * 64 + f * 8, 8), 8)

    def sweep_1(k, previous):
        inv, low = inv_t[tile(k), :], low_t[tile(k), :]
        current = tuple(av[at_level(k, f), :] * inv + low * previous[f] for f in range(TRC))
        for f in range(TRC):
            av[at_level(k, f), :] = current[f]
        return current

    lax.fori_loop(0, LEV, sweep_1, (zero,) * TRC, unroll=4)
    second, third = cst[...] >= 2, cst[...] >= 3

    def sweep_2(i, carry):
        following, previous = carry
        k = LEV - 1 - i
        up = up_t[tile(k), :]
        inv = jnp.where(second, inv_b[tile(k), :], 1.0)
        low = jnp.where(second, low_b[tile(k), :], 0.0)
        solved = tuple(av[at_level(k, f), :] + up * following[f] for f in range(TRC))
        current = tuple(solved[f] * inv + low * previous[f] for f in range(TRC))
        for f in range(TRC):
            av[at_level(k, f), :] = current[f]
        return solved, current

    lax.fori_loop(0, LEV, sweep_2, ((zero,) * TRC, (zero,) * TRC), unroll=4)

    def sweep_3(k, carry):
        following, previous = carry
        up = jnp.where(second, up_b[tile(k), :], 0.0)
        inv = jnp.where(third, inv_t[tile(k), :], 1.0)
        low = jnp.where(third, low_t[tile(k), :], 0.0)
        solved = tuple(av[at_level(k, f), :] + up * following[f] for f in range(TRC))
        current = tuple(solved[f] * inv + low * previous[f] for f in range(TRC))
        for f in range(TRC):
            av[at_level(k, f), :] = current[f]
        return solved, current

    lax.fori_loop(0, LEV, sweep_3, ((zero,) * TRC, (zero,) * TRC), unroll=4)

    slots = iota((16, 128), 0)
    for f in range(TRC):
        base = av[(LEV - 1) * 64 + f * 8 : (LEV - 1) * 64 + f * 8 + 8, :]
        rest = base - base.astype(BF16).astype(F32)
        for x in range(8):
            hit = jnp.broadcast_to(rank[x : x + 1, :], (16, 128)) == slots
            for part, value in enumerate((base, rest)):
                spread[part * 128 + f * 16 : part * 128 + f * 16 + 16, x * 128 : x * 128 + 128] = jnp.where(
                    hit, jnp.broadcast_to(value[x : x + 1, :], (16, 128)), 0.0
                ).astype(BF16)
    placed = lax.dot_general(
        chosen_by[:ALL, :], spread[...], (((1,), (1,)), ((), ())), preferred_element_type=F32
    )
    sb[...] = placed[:, :128] + placed[:, 128:]
    own_bottom = pltpu.make_async_copy(sb.at[me], rbm.at[me], bo)
    own_bottom.start()

    def send_bottom(p, where):
        pltpu.make_async_remote_copy(
            sb.at[p], rbm.at[me], bs, br, device_id=where, device_id_type=MESH
        ).start()

    for_peers(send_bottom)

    def sweep_4(i, following):
        k = LEV - 1 - i
        up = jnp.where(third, up_t[tile(k), :], 0.0)
        solved = tuple(av[at_level(k, f), :] + up * following[f] for f in range(TRC))
        for f in range(TRC):
            out[at_level(k, f), :] = solved[f]
        return solved

    lax.fori_loop(0, LEV, sweep_4, (zero,) * TRC, unroll=4)

    own_bottom.wait()
    sized = rbm.at[pl.ds(0, ALL - 1)]
    pltpu.make_async_copy(sized, sized, br).wait()
    for pair in row_copies:
        for copy in pair:
            copy.wait_send()
    sized = xb.at[pl.ds(0, ALL - 1), pl.ds(0, 9)]
    pltpu.make_async_copy(sized, sized, ks).wait()
    sized = sb.at[pl.ds(0, ALL - 1)]
    pltpu.make_async_copy(sized, sized, bs).wait()


def finish(mixed, received, out, bot, held, sem):
    part = ROWS // 8
    copies = [
        pltpu.make_async_copy(mixed.at[pl.ds(i * part, part)], out.at[pl.ds(i * part, part)], sem.at[i])
        for i in range(8)
    ]
    for copy in copies:
        copy.start()
    for t in range(16):
        held[pl.ds(t, 8, stride=16), :] = swap_blocks(received[t * 8 : t * 8 + 8, :])
    copies.append(pltpu.make_async_copy(held, bot, sem.at[8]))
    copies[-1].start()
    for copy in copies:
        copy.wait()


def shards(tracers, wind_east, wind_north, point_mass, diffusivity, destination, column_cost):
    weights = jnp.asarray(north_weights())
    vmem = pltpu.VMEM
    dma = pltpu.SemaphoreType.DMA
    operands = (
        tracers.reshape(ROWS, 128),
        wind_east.reshape(LEV * 8, 128),
        wind_north.reshape(LEV * 8, 128),
        point_mass,
        diffusivity.reshape(LEV * 16, 128),
        destination.reshape(8, 128),
        column_cost.reshape(8, 128),
        weights,
    )
    mixed, received = pl.pallas_call(
        kernel,
        out_shape=[vmem((ROWS, 128), F32), vmem((128, 128), F32)],
        in_specs=[pl.BlockSpec(memory_space=pltpu.HBM)] * 8,
        out_specs=[pl.BlockSpec(memory_space=vmem)] * 2,
        scratch_shapes=[
            vmem((ROWS, 128), F32),
            vmem((LEV * 8, 128), F32),
            vmem((LEV * 8, 128), F32),
            vmem((8, 128), F32),
            vmem((LEV * 16, 128), F32),
            vmem((8, 128), jnp.int32),
            vmem((8, 128), jnp.int32),
            vmem((256, 256), BF16),
            vmem((ALL, 16, 128), F32),
            vmem((ALL, 16, 128), F32),
            vmem((LEV + 1, 8, 8, 128), F32),
            vmem((2, LEV + 1, 8, 128), F32),
            vmem((2, 8, 8, 128), F32),
            vmem((2, 8, 8, 128), F32),
            vmem((4, 8, 128), F32),
            vmem((2, 8, 8, 128), F32),
            vmem((8, 8, 128), F32),
            vmem((ROWS, 128), F32),
            vmem((8, 128), jnp.int32),
            vmem((2 * ALL, 1024), BF16),
            vmem((LEV * 16, 2 * ALL), BF16),
            vmem((256, 1024), BF16),
            vmem((LEV * 8, 128), F32),
        ]
        + [vmem((LEV * 8, 128), F32)] * 6
        + [vmem((128, 128), F32)]
        + [dma((8,)), dma, dma, dma, dma((2, 3)), dma((2, 3)), dma((2,)), dma((2,)), dma((4,)), dma((4,)), dma, dma, dma],
        compiler_params=pltpu.CompilerParams(
            collective_id=0, has_side_effects=True, vmem_limit_bytes=48 * 2**20
        ),
        cost_estimate=pl.CostEstimate(flops=2 * 10**9, bytes_accessed=7 * 10**6, transcendentals=0),
        name="tracer_step",
    )(*(pltpu.with_memory_space_constraint(value, pltpu.HBM) for value in operands))
    mixed, bottoms = pl.pallas_call(
        finish,
        out_shape=[jax.ShapeDtypeStruct((ROWS, 128), F32), jax.ShapeDtypeStruct((128, 128), F32)],
        in_specs=[pl.BlockSpec(memory_space=vmem)] * 2,
        out_specs=[pl.BlockSpec(memory_space=pltpu.HBM)] * 2,
        scratch_shapes=[vmem((128, 128), F32), dma((9,))],
        cost_estimate=pl.CostEstimate(flops=0, bytes_accessed=5 * 10**6, transcendentals=0),
        compiler_params=pltpu.CompilerParams(vmem_limit_bytes=8 * 2**20),
        name="write_out",
    )(*(pltpu.with_memory_space_constraint(value, vmem) for value in (mixed, received)))
    return mixed.reshape(LEV, TRC, 8, 128), bottoms.reshape(TRC, 1, ALL * 16)


def solution(mesh):
    return jax.shard_map(
        shards,
        mesh=mesh,
        in_specs=(
            P(None, None, "grp", "dev"),
            P(None, "grp", "dev"),
            P(None, "grp", "dev"),
            P("grp", "dev"),
            P(None, ("grp", "dev"), None),
            P(("grp", "dev"), None, None),
            P(("grp", "dev"), None),
        ),
        out_specs=(P(None, None, "grp", "dev"), P(None, ("grp", "dev"), None)),
        check_vma=False,
    )
```

```python
import jax
import jax.numpy as jnp
import numpy as np
from jax import lax
from jax.experimental import pallas as pl
from jax.experimental.pallas import tpu as pltpu
from jax.sharding import PartitionSpec as P

LEV = 72
TRC = 8
ROWS = LEV * TRC * 8
GRP = 4
DEV = 32
ALL = GRP * DEV
CUTS = ((0, 25), (25, 49), (49, 73))
MESH = pl.DeviceIdType.MESH
F32 = jnp.float32
BF16 = jnp.bfloat16


def gll_derivative():
    points = np.array([-1.0, -1.0 / np.sqrt(5.0), 1.0 / np.sqrt(5.0), 1.0])
    der = np.zeros((4, 4))
    for i in range(4):
        for k in range(4):
            others = [m for m in range(4) if m != k]
            if i == k:
                der[i, k] = sum(1.0 / (points[k] - points[m]) for m in others)
            else:
                term = 1.0
                for m in others:
                    if m != i:
                        term *= (points[i] - points[m]) / (points[k] - points[m])
                der[i, k] = term / (points[k] - points[i])
    return der


def north_weights():
    along = np.kron(np.eye(32), gll_derivative().T).astype(np.float32)
    high = along.astype(jnp.bfloat16)
    low = (along - high.astype(np.float32)).astype(jnp.bfloat16)
    return np.block([[high, low], [high, np.zeros_like(low)]])


def iota(shape, dim):
    return lax.broadcasted_iota(jnp.int32, shape, dim)


def swap_blocks(values, last=False):
    row, lane = iota((8, 128), 0), iota((8, 128), 1)
    turned = pltpu.roll(values, 0, 1, stride=16, stride_axis=0)
    moved = jnp.take_along_axis(turned, (lane // 16 - row + 8) % 8, axis=0, mode="promise_in_bounds")
    source = lane % 8 * 16 + lane // 8 if last else lane
    return jnp.take_along_axis(moved, (source + 16 * row) % 128, axis=1, mode="promise_in_bounds")


def halves(values):
    high = values.astype(BF16)
    return high, (values - high.astype(F32)).astype(BF16)


def kernel(
    tr_h, we_h, wn_h, pm_h, df_h, dst_h, cst_h, w_h, out, rbm,
    tr, we, wn, pm, df, dst, cst, w, xb, rb, vb, hx, acc, hy, hd, uh, av, rank, chosen_by, lhs, spread, kc,
    inv_t, low_t, up_t, inv_b, low_b, up_b, sb,
    local_sem, ks, kr, ko, hs, hr, ys, yr, ds, dr, bs, br, bo,
):
    g, d = lax.axis_index("grp"), lax.axis_index("dev")
    me = g * DEV + d
    der = gll_derivative().astype(np.float32)

    z, y, core = lax.div(d, 8), lax.rem(lax.div(d, 2), 4), lax.rem(d, 2)

    def eight(step, t, act, count=8):
        to_g, to_z = lax.rem(g + step, GRP), lax.rem(z + t + 1, 4)
        for i in range(count):
            to_d = to_z * 8 + lax.rem(y + i // 2 + 1, 4) * 2 + lax.rem(core + i + 1, 2)
            act(to_g * DEV + to_d, (to_g, to_d))

    def for_peers(act, steps=(2, 1, 3, 0), beside=None):
        for turn, step in enumerate(steps):

            def some(t, carry):
                eight(step, 2 * t, act)
                eight(step, 2 * t + 1, act)
                if beside is not None:
                    beside(2 * turn + t)
                return carry

            lax.fori_loop(0, 1 if step == 0 else 2, some, 0)
            if step == 0:
                eight(0, 2, act)
                eight(0, 3, act, 7)
                if beside is not None:
                    beside(2 * turn + 1)

    loads = [
        pltpu.make_async_copy(src, dst_ref, local_sem.at[i])
        for i, (src, dst_ref) in enumerate(
            ((df_h, df), (tr_h, tr), (we_h, we), (wn_h, wn), (pm_h, pm), (w_h, w), (dst_h, dst), (cst_h, cst))
        )
    ]
    for copy in loads:
        copy.start()

    barrier = pltpu.get_barrier_semaphore()

    def greet(p, where):
        pl.semaphore_signal(barrier, inc=1, device_id=where, device_id_type=MESH)

    for_peers(greet, (2, 1))

    loads[0].wait()
    xb2, rb2 = xb.reshape(ALL * 16, 128), rb.reshape(ALL * 16, 128)

    def pack(tile):
        for group in range(9):
            rows = df[pl.ds(group * 128 + tile, 8, stride=16), :]
            xb2[pl.ds(tile * 128 + group, 8, stride=16), :] = swap_blocks(rows, last=True)

    def pack_four(part):
        for i in range(4):
            pack(4 * part + i)

    for_peers(greet, (3, 0), pack_four)
    own = pltpu.make_async_copy(xb.at[me, pl.ds(0, 9)], rb.at[me, pl.ds(0, 9)], ko)
    own.start()

    def send_kappa(p, where):
        pltpu.make_async_remote_copy(
            xb.at[p, pl.ds(0, 9)], rb.at[me, pl.ds(0, 9)], ks, kr, device_id=where, device_id_type=MESH
        ).start()

    for copy in loads[1:]:
        copy.wait()
    pl.semaphore_wait(barrier, ALL - 1)
    for x in range(8):
        vb[0, x] = jnp.broadcast_to(pm[x : x + 1, :], (8, 128))

    def advect(block):
        first = block * 8
        cells = [
            [tr[pl.ds((first + j) * 64 + x, 8, stride=8), :] for x in range(8)] for j in range(8)
        ]
        stacked = jnp.concatenate([c for level in cells for c in level], axis=0)
        product = jnp.dot(jnp.concatenate(halves(stacked), axis=1), w[...], preferred_element_type=F32)
        north = product[:, :128] + product[:, 128:]
        for j in range(8):
            for x in range(8):
                base = x // 4 * 4
                east = sum(float(der[x % 4, k]) * cells[j][base + k] for k in range(4))
                at = pl.ds((first + j) * 8 + x, 1)
                row = (j * 8 + x) * 8
                moved = cells[j][x] - (we[at, :] * east + wn[at, :] * north[row : row + 8])
                vb[1 + first + j, x] = pm[x : x + 1, :] * moved

    for_peers(send_kappa, beside=advect)
    advect(8)

    lane = iota((8, 128), 1)
    zero = jnp.zeros((8, 128), F32)

    def gather_edges(x, carry):
        first = last = zero
        for s in range(LEV + 1):
            value = pltpu.roll(vb[s, x], s + 1, 1)
            first = jnp.where(lane == s + 1, value, first)
            last = jnp.where(lane == s, value, last)
        acc[0, x] = first
        acc[1, x] = last
        return carry

    lax.fori_loop(0, 8, gather_edges, 0)
    up_g, down_g = lax.rem(g + 1, GRP), lax.rem(g + GRP - 1, GRP)
    up_d, down_d = lax.rem(d + 1, DEV), lax.rem(d + DEV - 1, DEV)
    edge_copies = [
        pltpu.make_async_remote_copy(src, to, s, r, device_id=where, device_id_type=MESH)
        for src, to, s, r, where in (
            (acc.at[1], hy.at[0], ys.at[0], yr.at[0], (g, up_d)),
            (acc.at[0], hy.at[1], ys.at[1], yr.at[1], (g, down_d)),
            (acc.at[1, 7], hd.at[0], ds.at[0], dr.at[0], (up_g, up_d)),
            (acc.at[1, 0], hd.at[1], ds.at[1], dr.at[1], (down_g, up_d)),
            (acc.at[0, 7], hd.at[2], ds.at[2], dr.at[2], (up_g, down_d)),
            (acc.at[0, 0], hd.at[3], ds.at[3], dr.at[3], (down_g, down_d)),
        )
    ]
    for copy in edge_copies:
        copy.start()
    row_copies = [
        [
            pltpu.make_async_remote_copy(
                vb.at[pl.ds(lo, hi - lo), x], hx.at[side, pl.ds(lo, hi - lo)], hs.at[side, part], hr.at[side, part],
                device_id=(to_g, d), device_id_type=MESH,
            )
            for side, (x, to_g) in enumerate(((7, up_g), (0, down_g)))
        ]
        for part, (lo, hi) in enumerate(CUTS)
    ]
    for pair in row_copies:
        for copy in pair:
            copy.start()

    devices = iota((ALL, 128), 0)
    earlier = jnp.concatenate(
        [(iota((128, 128), 0) < iota((128, 128), 1)).astype(F32), jnp.ones((128, 128), F32)], axis=1
    ).astype(BF16)
    before = jnp.zeros((ALL, 128), F32)
    for x in range(8):
        match = (jnp.broadcast_to(dst[x : x + 1, :], (ALL, 128)) == devices).astype(F32)
        chosen = match.astype(BF16)
        counts = jnp.dot(chosen, earlier, preferred_element_type=F32)
        order = jnp.sum((counts[:, :128] + before) * match, axis=0, keepdims=True)
        rank[x : x + 1, :] = order.astype(jnp.int32)
        at = slice(x * 128, x * 128 + 128)
        chosen_by[:ALL, at] = chosen
        chosen_by[ALL:, at] = chosen
        before = before + counts[:, 128:]

    at_first, at_last = lane % 4 == 0, lane % 4 == 3
    at_first, at_last = at_first & (lane > 0), at_last & (lane < 127)
    at_side = at_first | at_last

    def across(u):
        beside = jnp.where(at_first, pltpu.roll(u, 1, 1), pltpu.roll(u, 127, 1))
        return u + jnp.where(at_side, beside, 0.0)

    def put(s, x, value):
        av[pl.ds(s * 64 + x, 8, stride=8), :] = value

    def sum_inner(s, carry):
        middle = across(vb[s, 3] + vb[s, 4])
        put(s, 3, middle)
        put(s, 4, middle)
        for x in (1, 2, 5, 6):
            put(s, x, across(vb[s, x]))
        return carry

    lax.fori_loop(0, LEV + 1, sum_inner, 0, unroll=4)

    own.wait()
    sized = rb.at[pl.ds(0, ALL - 1), pl.ds(0, 9)]
    pltpu.make_async_copy(sized, sized, kr).wait()

    for group in range(9):
        values = rb2[pl.ds(group, ALL, stride=16), :].T
        lhs[group * 128 : group * 128 + 128, :] = jnp.concatenate(halves(values), axis=1)

    def columns(pair, carry):
        at = pl.ds(pl.multiple_of(pair * 256, 256), 256)
        found = jnp.dot(lhs[...], chosen_by[:, at], preferred_element_type=F32)
        for half in range(2):
            x = 2 * pair + half
            order = jnp.broadcast_to(rank[pl.ds(x, 1), :], (8, 128))
            hits = [order == r for r in range(16)]
            for group in range(9):
                value = found[group * 128 : group * 128 + 8, half * 128 : half * 128 + 128]
                for r in range(1, 16):
                    row = group * 128 + r * 8
                    value = jnp.where(hits[r], found[row : row + 8, half * 128 : half * 128 + 128], value)
                kc[pl.ds(group * 64 + x, 8, stride=8), :] = value
        return carry

    lax.fori_loop(0, 4, columns, 0)

    def tile(k):
        return pl.ds(pl.multiple_of(k * 8, 8), 8)

    def eliminate(i, carry):
        gain_t, h_t, gain_b, h_b = carry
        k = i
        kk = LEV - 1 - i
        next_t = jnp.where(k < LEV - 1, 0.5 * (kc[tile(k), :] + kc[tile(jnp.minimum(k + 1, LEV - 1)), :]), 0.0)
        e = 1.0 + gain_t
        inv = 1.0 / (e + next_t)
        inv_t[tile(k), :] = inv
        low_t[tile(k), :] = h_t * inv
        up = next_t * inv
        up_t[tile(k), :] = up
        next_b = jnp.where(kk > 0, 0.5 * (kc[tile(kk), :] + kc[tile(jnp.maximum(kk - 1, 0)), :]), 0.0)
        e_b = 1.0 + gain_b
        inv2 = 1.0 / (e_b + next_b)
        inv_b[tile(kk), :] = inv2
        low_b[tile(kk), :] = h_b * inv2
        up2 = next_b * inv2
        up_b[tile(kk), :] = up2
        return up * e, next_t, up2 * e_b, next_b

    lax.fori_loop(0, LEV, eliminate, (zero,) * 4, unroll=4)

    for part, (lo, hi) in enumerate(CUTS):
        for copy in row_copies[part]:
            copy.wait_recv()

        def sum_outer(s, carry):
            for side, x in ((0, 0), (1, 7)):
                put(s, x, across(vb[s, x] + hx[side, s]))
            return carry

        lax.fori_loop(lo, hi, sum_outer, 0, unroll=4)

    for copy in edge_copies:
        copy.wait()
    for side in range(2):
        middle = hy[side, 3] + hy[side, 4]
        hy[side, 0] = hy[side, 0] + hd[2 * side]
        hy[side, 7] = hy[side, 7] + hd[2 * side + 1]
        hy[side, 3] = middle
        hy[side, 4] = middle
    even, at_end = lane % 2 == 0, (lane == 0) | (lane == 127)
    hy2 = hy.reshape(2 * 64, 128)
    for f in range(TRC):
        from_left = hy2[pl.ds(f, 8, stride=8), :]
        from_right = pltpu.roll(hy2[pl.ds(64 + f, 8, stride=8), :], 126, 1)
        uh[0, f] = jnp.where(even, from_left, from_right)
        uh[1, f] = jnp.where(even, from_right, from_left)

    def whole(s, f):
        halo = pltpu.roll(uh[lax.rem(s, 2), f], lax.rem(128 - s, 128), 1)
        return av[pl.ds(pl.multiple_of(s * 64 + f * 8, 8), 8), :] + jnp.where(at_end, halo, 0.0)

    share = 1.0 / whole(jnp.int32(0), 0)

    def at_level(k, f):
        return pl.ds(pl.multiple_of((k + 1) * 64 + f * 8, 8), 8)

    def sweep_1(k, previous):
        inv, low = inv_t[tile(k), :], low_t[tile(k), :]
        inv = inv * share
        current = tuple(whole(k + 1, f) * inv + low * previous[f] for f in range(TRC))
        for f in range(TRC):
            av[at_level(k, f), :] = current[f]
        return current

    lax.fori_loop(0, LEV, sweep_1, (zero,) * TRC, unroll=4)
    second, third = cst[...] >= 2, cst[...] >= 3

    def sweep_2(i, carry):
        following, previous = carry
        k = LEV - 1 - i
        up = up_t[tile(k), :]
        inv = jnp.where(second, inv_b[tile(k), :], 1.0)
        low = jnp.where(second, low_b[tile(k), :], 0.0)
        solved = tuple(av[at_level(k, f), :] + up * following[f] for f in range(TRC))
        current = tuple(solved[f] * inv + low * previous[f] for f in range(TRC))
        for f in range(TRC):
            av[at_level(k, f), :] = current[f]
        return solved, current

    lax.fori_loop(0, LEV, sweep_2, ((zero,) * TRC, (zero,) * TRC), unroll=4)

    def sweep_3(k, carry):
        following, previous = carry
        up = jnp.where(second, up_b[tile(k), :], 0.0)
        inv = jnp.where(third, inv_t[tile(k), :], 1.0)
        low = jnp.where(third, low_t[tile(k), :], 0.0)
        solved = tuple(av[at_level(k, f), :] + up * following[f] for f in range(TRC))
        current = tuple(solved[f] * inv + low * previous[f] for f in range(TRC))
        for f in range(TRC):
            av[at_level(k, f), :] = current[f]
        return solved, current

    lax.fori_loop(0, LEV, sweep_3, ((zero,) * TRC, (zero,) * TRC), unroll=4)

    slots = iota((16, 128), 0)
    for f in range(TRC):
        base = av[LEV * 64 + f * 8 : LEV * 64 + f * 8 + 8, :]
        rest = base - base.astype(BF16).astype(F32)
        for x in range(8):
            hit = jnp.broadcast_to(rank[x : x + 1, :], (16, 128)) == slots
            for part, value in enumerate((base, rest)):
                spread[part * 128 + f * 16 : part * 128 + f * 16 + 16, x * 128 : x * 128 + 128] = jnp.where(
                    hit, jnp.broadcast_to(value[x : x + 1, :], (16, 128)), 0.0
                ).astype(BF16)
    placed = lax.dot_general(
        chosen_by[:ALL, :], spread[...], (((1,), (1,)), ((), ())), preferred_element_type=F32
    )
    sb[...] = placed[:, :128] + placed[:, 128:]
    own_bottom = pltpu.make_async_copy(sb.at[me], rbm.at[me], bo)
    own_bottom.start()

    def send_bottom(p, where):
        pltpu.make_async_remote_copy(
            sb.at[p], rbm.at[me], bs, br, device_id=where, device_id_type=MESH
        ).start()

    for_peers(send_bottom)

    def sweep_4(i, following):
        k = LEV - 1 - i
        up = jnp.where(third, up_t[tile(k), :], 0.0)
        solved = tuple(av[at_level(k, f), :] + up * following[f] for f in range(TRC))
        for f in range(TRC):
            out[pl.ds(pl.multiple_of(k * 64 + f * 8, 8), 8), :] = solved[f]
        return solved

    lax.fori_loop(0, LEV, sweep_4, (zero,) * TRC, unroll=4)

    own_bottom.wait()
    sized = rbm.at[pl.ds(0, ALL - 1)]
    pltpu.make_async_copy(sized, sized, br).wait()
    for pair in row_copies:
        for copy in pair:
            copy.wait_send()
    sized = xb.at[pl.ds(0, ALL - 1), pl.ds(0, 9)]
    pltpu.make_async_copy(sized, sized, ks).wait()
    sized = sb.at[pl.ds(0, ALL - 1)]
    pltpu.make_async_copy(sized, sized, bs).wait()


def finish(mixed, received, out, bot, held, sem):
    part = ROWS // 8
    copies = [
        pltpu.make_async_copy(mixed.at[pl.ds(i * part, part)], out.at[pl.ds(i * part, part)], sem.at[i])
        for i in range(8)
    ]
    for copy in copies:
        copy.start()
    for t in range(16):
        held[pl.ds(t, 8, stride=16), :] = swap_blocks(received[t * 8 : t * 8 + 8, :])
    copies.append(pltpu.make_async_copy(held, bot, sem.at[8]))
    copies[-1].start()
    for copy in copies:
        copy.wait()


def shards(tracers, wind_east, wind_north, point_mass, diffusivity, destination, column_cost):
    weights = jnp.asarray(north_weights())
    vmem = pltpu.VMEM
    dma = pltpu.SemaphoreType.DMA
    operands = (
        tracers.reshape(ROWS, 128),
        wind_east.reshape(LEV * 8, 128),
        wind_north.reshape(LEV * 8, 128),
        point_mass,
        diffusivity.reshape(LEV * 16, 128),
        destination.reshape(8, 128),
        column_cost.reshape(8, 128),
        weights,
    )
    mixed, received = pl.pallas_call(
        kernel,
        out_shape=[vmem((ROWS, 128), F32), vmem((128, 128), F32)],
        in_specs=[pl.BlockSpec(memory_space=pltpu.HBM)] * 8,
        out_specs=[pl.BlockSpec(memory_space=vmem)] * 2,
        scratch_shapes=[
            vmem((ROWS, 128), F32),
            vmem((LEV * 8, 128), F32),
            vmem((LEV * 8, 128), F32),
            vmem((8, 128), F32),
            vmem((LEV * 16, 128), F32),
            vmem((8, 128), jnp.int32),
            vmem((8, 128), jnp.int32),
            vmem((256, 256), BF16),
            vmem((ALL, 16, 128), F32),
            vmem((ALL, 16, 128), F32),
            vmem((LEV + 1, 8, 8, 128), F32),
            vmem((2, LEV + 1, 8, 128), F32),
            vmem((2, 8, 8, 128), F32),
            vmem((2, 8, 8, 128), F32),
            vmem((4, 8, 128), F32),
            vmem((2, 8, 8, 128), F32),
            vmem((ROWS + 64, 128), F32),
            vmem((8, 128), jnp.int32),
            vmem((2 * ALL, 1024), BF16),
            vmem((LEV * 16, 2 * ALL), BF16),
            vmem((256, 1024), BF16),
            vmem((LEV * 8, 128), F32),
        ]
        + [vmem((LEV * 8, 128), F32)] * 6
        + [vmem((128, 128), F32)]
        + [dma((8,)), dma, dma, dma, dma((2, 3)), dma((2, 3)), dma((2,)), dma((2,)), dma((4,)), dma((4,)), dma, dma, dma],
        compiler_params=pltpu.CompilerParams(
            collective_id=0, has_side_effects=True, vmem_limit_bytes=48 * 2**20
        ),
        cost_estimate=pl.CostEstimate(flops=2 * 10**9, bytes_accessed=7 * 10**6, transcendentals=0),
        name="tracer_step",
    )(*(pltpu.with_memory_space_constraint(value, pltpu.HBM) for value in operands))
    mixed, bottoms = pl.pallas_call(
        finish,
        out_shape=[jax.ShapeDtypeStruct((ROWS, 128), F32), jax.ShapeDtypeStruct((128, 128), F32)],
        in_specs=[pl.BlockSpec(memory_space=vmem)] * 2,
        out_specs=[pl.BlockSpec(memory_space=pltpu.HBM)] * 2,
        scratch_shapes=[vmem((128, 128), F32), dma((9,))],
        cost_estimate=pl.CostEstimate(flops=0, bytes_accessed=5 * 10**6, transcendentals=0),
        compiler_params=pltpu.CompilerParams(vmem_limit_bytes=8 * 2**20),
        name="write_out",
    )(*(pltpu.with_memory_space_constraint(value, vmem) for value in (mixed, received)))
    return mixed.reshape(LEV, TRC, 8, 128), bottoms.reshape(TRC, 1, ALL * 16)


def solution(mesh):
    return jax.shard_map(
        shards,
        mesh=mesh,
        in_specs=(
            P(None, None, "grp", "dev"),
            P(None, "grp", "dev"),
            P(None, "grp", "dev"),
            P("grp", "dev"),
            P(None, ("grp", "dev"), None),
            P(("grp", "dev"), None, None),
            P(("grp", "dev"), None),
        ),
        out_specs=(P(None, None, "grp", "dev"), P(None, ("grp", "dev"), None)),
        check_vma=False,
    )
```

```python
import jax
import jax.numpy as jnp
import numpy as np
from jax import lax
from jax.experimental import pallas as pl
from jax.experimental.pallas import tpu as pltpu
from jax.sharding import PartitionSpec as P

LEV = 72
TRC = 8
ROWS = LEV * TRC * 8
GRP = 4
DEV = 32
ALL = GRP * DEV
CUTS = ((0, 25), (25, 49), (49, 73))
MESH = pl.DeviceIdType.MESH
F32 = jnp.float32
BF16 = jnp.bfloat16


def gll_derivative():
    points = np.array([-1.0, -1.0 / np.sqrt(5.0), 1.0 / np.sqrt(5.0), 1.0])
    der = np.zeros((4, 4))
    for i in range(4):
        for k in range(4):
            others = [m for m in range(4) if m != k]
            if i == k:
                der[i, k] = sum(1.0 / (points[k] - points[m]) for m in others)
            else:
                term = 1.0
                for m in others:
                    if m != i:
                        term *= (points[i] - points[m]) / (points[k] - points[m])
                der[i, k] = term / (points[k] - points[i])
    return der


def north_weights():
    along = np.kron(np.eye(32), gll_derivative().T).astype(np.float32)
    high = along.astype(jnp.bfloat16)
    low = (along - high.astype(np.float32)).astype(jnp.bfloat16)
    return np.block([[high, low], [high, np.zeros_like(low)]])


def iota(shape, dim):
    return lax.broadcasted_iota(jnp.int32, shape, dim)


def swap_blocks(values, last=False):
    row, lane = iota((8, 128), 0), iota((8, 128), 1)
    turned = pltpu.roll(values, 0, 1, stride=16, stride_axis=0)
    moved = jnp.take_along_axis(turned, (lane // 16 - row + 8) % 8, axis=0, mode="promise_in_bounds")
    source = lane % 8 * 16 + lane // 8 if last else lane
    return jnp.take_along_axis(moved, (source + 16 * row) % 128, axis=1, mode="promise_in_bounds")


def halves(values):
    high = values.astype(BF16)
    return high, (values - high.astype(F32)).astype(BF16)


def kernel(
    tr_h, we_h, wn_h, pm_h, df_h, dst_h, cst_h, w_h, out, rbm,
    tr, we, wn, pm, df, dst, cst, w, xb, rb, vb, hx, acc, hy, hd, uh, av, rank, chosen_by, lhs, spread, kc,
    inv_t, low_t, up_t, inv_b, low_b, up_b, sb,
    local_sem, ks, kr, ko, hs, hr, ys, yr, ds, dr, bs, br, bo,
):
    g, d = lax.axis_index("grp"), lax.axis_index("dev")
    me = g * DEV + d
    der = gll_derivative().astype(np.float32)

    z, y, core = lax.div(d, 8), lax.rem(lax.div(d, 2), 4), lax.rem(d, 2)

    def eight(step, t, act, count=8):
        to_g, to_z = lax.rem(g + step, GRP), lax.rem(z + t + 1, 4)
        for i in range(count):
            to_d = to_z * 8 + lax.rem(y + i // 2 + 1, 4) * 2 + lax.rem(core + i + 1, 2)
            act(to_g * DEV + to_d, (to_g, to_d))

    def for_peers(act, steps=(2, 1, 3, 0), beside=None):
        for turn, step in enumerate(steps):

            def some(t, carry):
                eight(step, 2 * t, act)
                eight(step, 2 * t + 1, act)
                if beside is not None:
                    beside(2 * turn + t)
                return carry

            lax.fori_loop(0, 1 if step == 0 else 2, some, 0)
            if step == 0:
                eight(0, 2, act)
                eight(0, 3, act, 7)
                if beside is not None:
                    beside(2 * turn + 1)

    loads = [
        pltpu.make_async_copy(src, dst_ref, local_sem.at[i])
        for i, (src, dst_ref) in enumerate(
            ((df_h, df), (tr_h, tr), (we_h, we), (wn_h, wn), (pm_h, pm), (w_h, w), (dst_h, dst), (cst_h, cst))
        )
    ]
    for copy in loads:
        copy.start()

    barrier = pltpu.get_barrier_semaphore()

    def greet(p, where):
        pl.semaphore_signal(barrier, inc=1, device_id=where, device_id_type=MESH)

    for_peers(greet, (2, 1))

    loads[0].wait()
    xb2, rb2 = xb.reshape(ALL * 16, 128), rb.reshape(ALL * 16, 128)

    def pack(tile):
        for group in range(9):
            rows = df[pl.ds(group * 128 + tile, 8, stride=16), :]
            xb2[pl.ds(tile * 128 + group, 8, stride=16), :] = swap_blocks(rows, last=True)

    def pack_four(part):
        for i in range(4):
            pack(4 * part + i)

    for_peers(greet, (3, 0), pack_four)
    own = pltpu.make_async_copy(xb.at[me, pl.ds(0, 9)], rb.at[me, pl.ds(0, 9)], ko)
    own.start()

    def send_kappa(p, where):
        pltpu.make_async_remote_copy(
            xb.at[p, pl.ds(0, 9)], rb.at[me, pl.ds(0, 9)], ks, kr, device_id=where, device_id_type=MESH
        ).start()

    for copy in loads[1:]:
        copy.wait()
    pl.semaphore_wait(barrier, ALL - 1)
    for x in range(8):
        vb[0, x] = jnp.broadcast_to(pm[x : x + 1, :], (8, 128))

    def advect(block):
        first = block * 8
        cells = [
            [tr[pl.ds((first + j) * 64 + x, 8, stride=8), :] for x in range(8)] for j in range(8)
        ]
        stacked = jnp.concatenate([c for level in cells for c in level], axis=0)
        product = jnp.dot(jnp.concatenate(halves(stacked), axis=1), w[...], preferred_element_type=F32)
        north = product[:, :128] + product[:, 128:]
        for j in range(8):
            for x in range(8):
                base = x // 4 * 4
                east = sum(float(der[x % 4, k]) * cells[j][base + k] for k in range(4))
                at = pl.ds((first + j) * 8 + x, 1)
                row = (j * 8 + x) * 8
                moved = cells[j][x] - (we[at, :] * east + wn[at, :] * north[row : row + 8])
                vb[1 + first + j, x] = pm[x : x + 1, :] * moved

    for_peers(send_kappa, beside=advect)
    advect(8)

    lane = iota((8, 128), 1)
    zero = jnp.zeros((8, 128), F32)

    def gather_edges(x, carry):
        first = last = zero
        for s in range(LEV + 1):
            value = pltpu.roll(vb[s, x], s + 1, 1)
            first = jnp.where(lane == s + 1, value, first)
            last = jnp.where(lane == s, value, last)
        acc[0, x] = first
        acc[1, x] = last
        return carry

    lax.fori_loop(0, 8, gather_edges, 0)
    up_g, down_g = lax.rem(g + 1, GRP), lax.rem(g + GRP - 1, GRP)
    up_d, down_d = lax.rem(d + 1, DEV), lax.rem(d + DEV - 1, DEV)
    edge_copies = [
        pltpu.make_async_remote_copy(src, to, s, r, device_id=where, device_id_type=MESH)
        for src, to, s, r, where in (
            (acc.at[1], hy.at[0], ys.at[0], yr.at[0], (g, up_d)),
            (acc.at[0], hy.at[1], ys.at[1], yr.at[1], (g, down_d)),
            (acc.at[1, 7], hd.at[0], ds.at[0], dr.at[0], (up_g, up_d)),
            (acc.at[1, 0], hd.at[1], ds.at[1], dr.at[1], (down_g, up_d)),
            (acc.at[0, 7], hd.at[2], ds.at[2], dr.at[2], (up_g, down_d)),
            (acc.at[0, 0], hd.at[3], ds.at[3], dr.at[3], (down_g, down_d)),
        )
    ]
    for copy in edge_copies:
        copy.start()
    row_copies = [
        [
            pltpu.make_async_remote_copy(
                vb.at[pl.ds(lo, hi - lo), x], hx.at[side, pl.ds(lo, hi - lo)], hs.at[side, part], hr.at[side, part],
                device_id=(to_g, d), device_id_type=MESH,
            )
            for side, (x, to_g) in enumerate(((7, up_g), (0, down_g)))
        ]
        for part, (lo, hi) in enumerate(CUTS)
    ]
    for pair in row_copies:
        for copy in pair:
            copy.start()

    devices = iota((ALL, 128), 0)
    earlier = jnp.concatenate(
        [(iota((128, 128), 0) < iota((128, 128), 1)).astype(F32), jnp.ones((128, 128), F32)], axis=1
    ).astype(BF16)
    before = jnp.zeros((ALL, 128), F32)
    for x in range(8):
        match = (jnp.broadcast_to(dst[x : x + 1, :], (ALL, 128)) == devices).astype(F32)
        chosen = match.astype(BF16)
        counts = jnp.dot(chosen, earlier, preferred_element_type=F32)
        order = jnp.sum((counts[:, :128] + before) * match, axis=0, keepdims=True)
        rank[x : x + 1, :] = order.astype(jnp.int32)
        at = slice(x * 128, x * 128 + 128)
        chosen_by[:ALL, at] = chosen
        chosen_by[ALL:, at] = chosen
        before = before + counts[:, 128:]

    at_first, at_last = lane % 4 == 0, lane % 4 == 3
    at_first, at_last = at_first & (lane > 0), at_last & (lane < 127)
    at_side = at_first | at_last

    def across(u):
        beside = jnp.where(at_first, pltpu.roll(u, 1, 1), pltpu.roll(u, 127, 1))
        return u + jnp.where(at_side, beside, 0.0)

    def put(s, x, value):
        av[pl.ds(s * 64 + x, 8, stride=8), :] = value

    def sum_inner(s, carry):
        middle = across(vb[s, 3] + vb[s, 4])
        put(s, 3, middle)
        put(s, 4, middle)
        for x in (0, 1, 2, 5, 6, 7):
            put(s, x, across(vb[s, x]))
        return carry

    lax.fori_loop(0, LEV + 1, sum_inner, 0, unroll=4)

    own.wait()
    sized = rb.at[pl.ds(0, ALL - 1), pl.ds(0, 9)]
    pltpu.make_async_copy(sized, sized, kr).wait()

    for group in range(9):
        values = rb2[pl.ds(group, ALL, stride=16), :].T
        lhs[group * 128 : group * 128 + 128, :] = jnp.concatenate(halves(values), axis=1)

    def columns(pair, carry):
        at = pl.ds(pl.multiple_of(pair * 256, 256), 256)
        found = jnp.dot(lhs[...], chosen_by[:, at], preferred_element_type=F32)
        for half in range(2):
            x = 2 * pair + half
            order = jnp.broadcast_to(rank[pl.ds(x, 1), :], (8, 128))
            hits = [order == r for r in range(16)]
            for group in range(9):
                value = found[group * 128 : group * 128 + 8, half * 128 : half * 128 + 128]
                for r in range(1, 16):
                    row = group * 128 + r * 8
                    value = jnp.where(hits[r], found[row : row + 8, half * 128 : half * 128 + 128], value)
                kc[pl.ds(group * 64 + x, 8, stride=8), :] = value
        return carry

    lax.fori_loop(0, 4, columns, 0)

    for copy in edge_copies:
        copy.wait()
    for side in range(2):
        middle = hy[side, 3] + hy[side, 4]
        hy[side, 0] = hy[side, 0] + hd[2 * side]
        hy[side, 7] = hy[side, 7] + hd[2 * side + 1]
        hy[side, 3] = middle
        hy[side, 4] = middle
    even, at_end = lane % 2 == 0, (lane == 0) | (lane == 127)
    hy2 = hy.reshape(2 * 64, 128)
    for f in range(TRC):
        from_left = hy2[pl.ds(f, 8, stride=8), :]
        from_right = pltpu.roll(hy2[pl.ds(64 + f, 8, stride=8), :], 126, 1)
        uh[0, f] = jnp.where(even, from_left, from_right)
        uh[1, f] = jnp.where(even, from_right, from_left)

    def add_lanes(s):
        shift, parity = lax.rem(128 - s, 128), lax.rem(s, 2)
        for f in range(TRC):
            at = pl.ds(pl.multiple_of(s * 64 + f * 8, 8), 8)
            av[at, :] = av[at, :] + jnp.where(at_end, pltpu.roll(uh[parity, f], shift, 1), 0.0)

    def sum_outer(s):
        for side, x in ((0, 0), (1, 7)):
            at = pl.ds(s * 64 + x, 8, stride=8)
            av[at, :] = av[at, :] + across(hx[side, s])

    def tile(k):
        return pl.ds(pl.multiple_of(k * 8, 8), 8)

    def eliminate(i, carry):
        gain_t, h_t, gain_b, h_b = carry
        k = i
        kk = LEV - 1 - i
        next_t = jnp.where(k < LEV - 1, 0.5 * (kc[tile(k), :] + kc[tile(jnp.minimum(k + 1, LEV - 1)), :]), 0.0)
        e = 1.0 + gain_t
        inv = 1.0 / (e + next_t)
        inv_t[tile(k), :] = inv
        low_t[tile(k), :] = h_t * inv
        up = next_t * inv
        up_t[tile(k), :] = up
        next_b = jnp.where(kk > 0, 0.5 * (kc[tile(kk), :] + kc[tile(jnp.maximum(kk - 1, 0)), :]), 0.0)
        e_b = 1.0 + gain_b
        inv2 = 1.0 / (e_b + next_b)
        inv_b[tile(kk), :] = inv2
        low_b[tile(kk), :] = h_b * inv2
        up2 = next_b * inv2
        up_b[tile(kk), :] = up2
        return up * e, next_t, up2 * e_b, next_b


    def at_level(k, f):
        return pl.ds(pl.multiple_of((k + 1) * 64 + f * 8, 8), 8)

    for pair in row_copies:
        for copy in pair:
            copy.wait_recv()
    sum_outer(jnp.int32(0))
    add_lanes(jnp.int32(0))

    def complete(s, carry):
        sum_outer(s)
        add_lanes(s)
        return eliminate(s - 1, carry)

    lax.fori_loop(1, LEV + 1, complete, (zero,) * 4, unroll=4)
    share = 1.0 / av[:8, :]

    def sweep_1(k, previous):
        inv, low = inv_t[tile(k), :] * share, low_t[tile(k), :]
        current = tuple(av[at_level(k, f), :] * inv + low * previous[f] for f in range(TRC))
        for f in range(TRC):
            av[at_level(k, f), :] = current[f]
        return current

    lax.fori_loop(0, LEV, sweep_1, (zero,) * TRC, unroll=4)

    second, third = cst[...] >= 2, cst[...] >= 3

    def sweep_2(i, carry):
        following, previous = carry
        k = LEV - 1 - i
        up = up_t[tile(k), :]
        inv = jnp.where(second, inv_b[tile(k), :], 1.0)
        low = jnp.where(second, low_b[tile(k), :], 0.0)
        solved = tuple(av[at_level(k, f), :] + up * following[f] for f in range(TRC))
        current = tuple(solved[f] * inv + low * previous[f] for f in range(TRC))
        for f in range(TRC):
            av[at_level(k, f), :] = current[f]
        return solved, current

    lax.fori_loop(0, LEV, sweep_2, ((zero,) * TRC, (zero,) * TRC), unroll=4)

    def sweep_3(k, carry):
        following, previous = carry
        up = jnp.where(second, up_b[tile(k), :], 0.0)
        inv = jnp.where(third, inv_t[tile(k), :], 1.0)
        low = jnp.where(third, low_t[tile(k), :], 0.0)
        solved = tuple(av[at_level(k, f), :] + up * following[f] for f in range(TRC))
        current = tuple(solved[f] * inv + low * previous[f] for f in range(TRC))
        for f in range(TRC):
            av[at_level(k, f), :] = current[f]
        return solved, current

    lax.fori_loop(0, LEV, sweep_3, ((zero,) * TRC, (zero,) * TRC), unroll=4)

    slots = iota((16, 128), 0)
    for f in range(TRC):
        base = av[LEV * 64 + f * 8 : LEV * 64 + f * 8 + 8, :]
        rest = base - base.astype(BF16).astype(F32)
        for x in range(8):
            hit = jnp.broadcast_to(rank[x : x + 1, :], (16, 128)) == slots
            for part, value in enumerate((base, rest)):
                spread[part * 128 + f * 16 : part * 128 + f * 16 + 16, x * 128 : x * 128 + 128] = jnp.where(
                    hit, jnp.broadcast_to(value[x : x + 1, :], (16, 128)), 0.0
                ).astype(BF16)
    placed = lax.dot_general(
        chosen_by[:ALL, :], spread[...], (((1,), (1,)), ((), ())), preferred_element_type=F32
    )
    sb[...] = placed[:, :128] + placed[:, 128:]
    own_bottom = pltpu.make_async_copy(sb.at[me], rbm.at[me], bo)
    own_bottom.start()

    def send_bottom(p, where):
        pltpu.make_async_remote_copy(
            sb.at[p], rbm.at[me], bs, br, device_id=where, device_id_type=MESH
        ).start()

    for_peers(send_bottom)

    def sweep_4(i, following):
        k = LEV - 1 - i
        up = jnp.where(third, up_t[tile(k), :], 0.0)
        solved = tuple(av[at_level(k, f), :] + up * following[f] for f in range(TRC))
        for f in range(TRC):
            out[pl.ds(pl.multiple_of(k * 64 + f * 8, 8), 8), :] = solved[f]
        return solved

    lax.fori_loop(0, LEV, sweep_4, (zero,) * TRC, unroll=4)

    own_bottom.wait()
    sized = rbm.at[pl.ds(0, ALL - 1)]
    pltpu.make_async_copy(sized, sized, br).wait()
    for pair in row_copies:
        for copy in pair:
            copy.wait_send()
    sized = xb.at[pl.ds(0, ALL - 1), pl.ds(0, 9)]
    pltpu.make_async_copy(sized, sized, ks).wait()
    sized = sb.at[pl.ds(0, ALL - 1)]
    pltpu.make_async_copy(sized, sized, bs).wait()


def finish(mixed, received, out, bot, held, sem):
    part = ROWS // 8
    copies = [
        pltpu.make_async_copy(mixed.at[pl.ds(i * part, part)], out.at[pl.ds(i * part, part)], sem.at[i])
        for i in range(8)
    ]
    for copy in copies:
        copy.start()
    for t in range(16):
        held[pl.ds(t, 8, stride=16), :] = swap_blocks(received[t * 8 : t * 8 + 8, :])
    copies.append(pltpu.make_async_copy(held, bot, sem.at[8]))
    copies[-1].start()
    for copy in copies:
        copy.wait()


def shards(tracers, wind_east, wind_north, point_mass, diffusivity, destination, column_cost):
    weights = jnp.asarray(north_weights())
    vmem = pltpu.VMEM
    dma = pltpu.SemaphoreType.DMA
    operands = (
        tracers.reshape(ROWS, 128),
        wind_east.reshape(LEV * 8, 128),
        wind_north.reshape(LEV * 8, 128),
        point_mass,
        diffusivity.reshape(LEV * 16, 128),
        destination.reshape(8, 128),
        column_cost.reshape(8, 128),
        weights,
    )
    mixed, received = pl.pallas_call(
        kernel,
        out_shape=[vmem((ROWS, 128), F32), vmem((128, 128), F32)],
        in_specs=[pl.BlockSpec(memory_space=pltpu.HBM)] * 8,
        out_specs=[pl.BlockSpec(memory_space=vmem)] * 2,
        scratch_shapes=[
            vmem((ROWS, 128), F32),
            vmem((LEV * 8, 128), F32),
            vmem((LEV * 8, 128), F32),
            vmem((8, 128), F32),
            vmem((LEV * 16, 128), F32),
            vmem((8, 128), jnp.int32),
            vmem((8, 128), jnp.int32),
            vmem((256, 256), BF16),
            vmem((ALL, 16, 128), F32),
            vmem((ALL, 16, 128), F32),
            vmem((LEV + 1, 8, 8, 128), F32),
            vmem((2, LEV + 1, 8, 128), F32),
            vmem((2, 8, 8, 128), F32),
            vmem((2, 8, 8, 128), F32),
            vmem((4, 8, 128), F32),
            vmem((2, 8, 8, 128), F32),
            vmem((ROWS + 64, 128), F32),
            vmem((8, 128), jnp.int32),
            vmem((2 * ALL, 1024), BF16),
            vmem((LEV * 16, 2 * ALL), BF16),
            vmem((256, 1024), BF16),
            vmem((LEV * 8, 128), F32),
        ]
        + [vmem((LEV * 8, 128), F32)] * 6
        + [vmem((128, 128), F32)]
        + [dma((8,)), dma, dma, dma, dma((2, 3)), dma((2, 3)), dma((2,)), dma((2,)), dma((4,)), dma((4,)), dma, dma, dma],
        compiler_params=pltpu.CompilerParams(
            collective_id=0, has_side_effects=True, vmem_limit_bytes=48 * 2**20
        ),
        cost_estimate=pl.CostEstimate(flops=2 * 10**9, bytes_accessed=7 * 10**6, transcendentals=0),
        name="tracer_step",
    )(*(pltpu.with_memory_space_constraint(value, pltpu.HBM) for value in operands))
    mixed, bottoms = pl.pallas_call(
        finish,
        out_shape=[jax.ShapeDtypeStruct((ROWS, 128), F32), jax.ShapeDtypeStruct((128, 128), F32)],
        in_specs=[pl.BlockSpec(memory_space=vmem)] * 2,
        out_specs=[pl.BlockSpec(memory_space=pltpu.HBM)] * 2,
        scratch_shapes=[vmem((128, 128), F32), dma((9,))],
        cost_estimate=pl.CostEstimate(flops=0, bytes_accessed=5 * 10**6, transcendentals=0),
        compiler_params=pltpu.CompilerParams(vmem_limit_bytes=8 * 2**20),
        name="write_out",
    )(*(pltpu.with_memory_space_constraint(value, vmem) for value in (mixed, received)))
    return mixed.reshape(LEV, TRC, 8, 128), bottoms.reshape(TRC, 1, ALL * 16)


def solution(mesh):
    return jax.shard_map(
        shards,
        mesh=mesh,
        in_specs=(
            P(None, None, "grp", "dev"),
            P(None, "grp", "dev"),
            P(None, "grp", "dev"),
            P("grp", "dev"),
            P(None, ("grp", "dev"), None),
            P(("grp", "dev"), None, None),
            P(("grp", "dev"), None),
        ),
        out_specs=(P(None, None, "grp", "dev"), P(None, ("grp", "dev"), None)),
        check_vma=False,
    )
```
